128 devices in a mesh: row: 32 (over z, y, x_hi), col: 4 (over x_lo, core).
Axes of the slice: x: 4 (x_hi: 2, x_lo: 2; x = x_hi * 2 + x_lo), y: 4, z: 4, core: 2. Of those that a mesh axis runs over, the one named last changes fastest.
Arguments:
- pair_block: bfloat16 [2048, 2048, 128], P('row', 'col'), may hold values from -6 to 6
- left_panel: bfloat16 [2048, 64, 128], P('row', 'col'), may hold values from -6 to 6
- right_panel: bfloat16 [2048, 64, 128], P('row', 'col'), may hold values from -6 to 6
- ln_gain: float32 [128], replicated, may hold values from 0.1 to 1.9
- ln_bias: float32 [128], replicated, may hold values from -3 to 3
- w_left: bfloat16 [128, 256], replicated, may hold values from -0.5 to 0.5
- w_right: bfloat16 [128, 256], replicated, may hold values from -0.5 to 0.5
- w_gate: bfloat16 [128, 128], replicated, may hold values from -0.5 to 0.5
- out_gain: float32 [128], replicated, may hold values from 0.1 to 1.9
- out_bias: float32 [128], replicated, may hold values from -3 to 3
- w_out: bfloat16 [128, 128], replicated, may hold values from -0.5 to 0.5
Outputs:
- update: bfloat16 [2048, 2048, 128], P('row', 'col')
The draws below stay inside these ranges and needn't reach their ends.
All inputs are finite; a program needn't handle non-finite values.
Results may differ from the reference program's by a relative error of at most 0.0065.
Values may be sent and summed in bfloat16 or wider, within the bound.
No kernel may reach another device: no remote copies, remote signals or barrier semaphores. Data moves between devices by JAX's collectives and lax.ppermute only.
A program may use at most 192 MiB of HBM per device.

```python
import jax
import jax.numpy as jnp
from jax import lax

C = 128
H = 128
K = 64
ROWS_DEV = 64
R = 2048
NJ = 2048


def steps_of(key, dims, split, least, largest):
    factor_of, own = 1.0, jax.random.fold_in(key, 6)
    for dim, parts in split:
        heights = jnp.exp(jax.random.uniform(jax.random.fold_in(own, dim), (parts,), jnp.float32, least / len(split), largest / len(split)))
        factor_of = factor_of * jnp.repeat(heights, dims[dim] // parts).reshape([-1 if axis == dim else 1 for axis in range(len(dims))])
    return factor_of


def normal_values(own_key, dims, width, bound, shards=(), held_as=jnp.bfloat16):
    drawn = jax.random.normal(own_key, dims, jnp.float32) * width
    if len(shards) > 0:
        drawn = steps_of(own_key, dims, shards, -0.22, 0.18) * drawn
    return jnp.clip(drawn, min=-bound, max=bound).astype(held_as)


def setup_inputs(seed: int = 0) -> dict:
    keys = jax.random.split(jax.random.key(seed), 12)
    pair_block = normal_values(keys[0], (R, NJ, C), 1.0, 6.0, ((0, 32), (1, 4)))
    left_panel = normal_values(keys[1], (R, K, C), 1.0, 6.0, ((0, 32), (1, 4)))
    right_panel = normal_values(keys[2], (NJ, K, C), 1.0, 6.0, ((0, 32), (1, 4)))
    ln_gain = jnp.clip(1.0 + 0.18 * jax.random.normal(keys[3], (C,), jnp.float32), 0.1, 1.9)
    ln_bias = normal_values(keys[4], (C,), 0.5, 3.0, (), jnp.float32)
    w_left = normal_values(keys[5], (C, 2 * H), C ** -0.5, 0.5)
    w_right = normal_values(keys[6], (C, 2 * H), C ** -0.5, 0.5)
    w_gate = normal_values(keys[7], (C, C), C ** -0.5, 0.5)
    out_gain = jnp.clip(1.0 + 0.18 * jax.random.normal(keys[8], (H,), jnp.float32), 0.1, 1.9)
    out_bias = normal_values(keys[9], (H,), 0.5, 3.0, (), jnp.float32)
    w_out = normal_values(keys[10], (H, C), H ** -0.5, 0.5)
    return dict(pair_block=pair_block, left_panel=left_panel, right_panel=right_panel, ln_gain=ln_gain, ln_bias=ln_bias, w_left=w_left, w_right=w_right, w_gate=w_gate, out_gain=out_gain, out_bias=out_bias, w_out=w_out)


def layer_norm(values, gain, bias):
    values = values.astype(jnp.float32)
    mean = lax.optimization_barrier(jnp.mean(values, axis=-1, keepdims=True))
    centered = values - mean
    var = lax.optimization_barrier(jnp.mean(centered * centered, axis=-1, keepdims=True))
    return centered / jnp.sqrt(var + 1e-05) * gain + bias

def project_panel(panel, weight, ln_gain, ln_bias):
    normed = layer_norm(panel, ln_gain, ln_bias).astype(jnp.bfloat16)
    proj = jnp.einsum('rkc,ch->rkh', normed.astype(jnp.float32), weight.astype(jnp.float32))
    half = weight.shape[1] // 2
    return (jax.nn.sigmoid(proj[..., :half]) * proj[..., half:]).astype(jnp.bfloat16)

def reference(pair_block, left_panel, right_panel, ln_gain, ln_bias, w_left, w_right, w_gate, out_gain, out_bias, w_out):
    left = project_panel(left_panel, w_left, ln_gain, ln_bias)
    right = project_panel(right_panel, w_right, ln_gain, ln_bias).astype(jnp.float32)
    blocks = R // ROWS_DEV
    left_blocks = left.reshape(blocks, ROWS_DEV, K, H)
    pair_blocks = pair_block.reshape(blocks, ROWS_DEV, NJ, C)

    def one_block(items):
        left_rows, pair_rows = items
        product = jnp.einsum('ikh,jkh->ijh', left_rows.astype(jnp.float32), right)
        normed = layer_norm(product, out_gain, out_bias).astype(jnp.bfloat16)
        norm_pair = layer_norm(pair_rows, ln_gain, ln_bias).astype(jnp.bfloat16)
        gate = jax.nn.sigmoid(jnp.einsum('ijc,cd->ijd', norm_pair.astype(jnp.float32), w_gate.astype(jnp.float32)))
        output = jnp.einsum('ijh,hc->ijc', normed.astype(jnp.float32), w_out.astype(jnp.float32))
        return (gate * output).astype(jnp.bfloat16)
    update = lax.map(one_block, (left_blocks, pair_blocks))
    return update.reshape(R, NJ, C)
```

```python
import functools

import jax
import jax.numpy as jnp
import numpy as np
from jax import lax
from jax.experimental import pallas as pl
from jax.experimental.pallas import tpu as pltpu
from jax.sharding import PartitionSpec as P

AXES = ("row", "col")
BF16, F32 = jnp.bfloat16, jnp.float32
DEVICES = [(z, y, x, c) for z in range(4) for y in range(4) for x in range(2) for c in range(4)]
MIB = 1 << 20


def device_id(z, y, x, c):
    return (((z % 4) * 4 + y % 4) * 2 + x % 2) * 4 + c


def move(value, dz=0, dy=0, dx=0):
    pairs = [(device_id(z, y, x, c), device_id(z + dz, y + dy, x + dx, c)) for z, y, x, c in DEVICES]
    return lax.ppermute(value, AXES, pairs)


def layer_norm(values, gain, bias):
    mean = jnp.mean(values, axis=-1, keepdims=True)
    centered = values - mean
    var = jnp.mean(centered * centered, axis=-1, keepdims=True)
    return centered * lax.rsqrt(var + 1e-05) * gain + bias


def sigmoid(values):
    return 0.5 * jnp.tanh(0.5 * values) + 0.5


def hidden_order():
    order = []
    for group in range(32):
        first = 2 * group
        order += [first, first + 64, first + 1, first + 65]
    return np.array(order)


def project_16(normed, weight, swap, store):
    proj = lax.dot_general(
        weight, normed.reshape(16 * 64, 128), (((0,), (1,)), ((), ())), preferred_element_type=F32
    )
    value = (sigmoid(proj[:128]) * proj[128:]).astype(BF16).astype(F32)
    low, high = value[:64], value[64:]
    lane = lax.broadcasted_iota(jnp.int32, (64, 128), 1)
    for pair in range(8):
        lo = low[:, pair * 128 : (pair + 1) * 128]
        hi = high[:, pair * 128 : (pair + 1) * 128]
        swap[:, 2 * pair, :] = jnp.where(lane < 64, lo, pltpu.roll(hi, 64, 1))
        swap[:, 2 * pair + 1, :] = jnp.where(lane < 64, pltpu.roll(lo, 64, 1), hi)
    for h in range(64):
        store(h, swap[h].astype(BF16))


def right_kernel(z_ref, p0, p1, p2, p3, gain, bias, weight, a_ref, b_ref, normed, swap):
    z = z_ref[0]
    for s, piece in enumerate((p0, p1, p2, p3)):
        start = pl.multiple_of(lax.rem(z - s + 4, 4) * 16, 16)
        normed[:, pl.ds(start, 16), :] = layer_norm(
            piece[...].astype(F32), gain[...], bias[...]
        ).astype(BF16)

    def store(h, tile):
        ref = a_ref if h < 32 else b_ref
        ref[:, (h % 32) * 128 : (h % 32 + 1) * 128] = tile

    project_16(normed[...], weight[...], swap, store)


def left_kernel(left, gain, bias, weight, spread, out, normed, swap, rows):
    for quarter in range(4):
        at = slice(quarter * 16, quarter * 16 + 16)
        for c in range(4):
            normed[:, c * 16 : (c + 1) * 16, :] = layer_norm(
                left[c, at].astype(F32), gain[...], bias[...]
            ).astype(BF16)

        def store(h, tile, at=at):
            rows[at, h * 128 : (h + 1) * 128] = tile

        project_16(normed[...], weight[...], swap, store)
    row = lax.broadcasted_iota(jnp.int32, (256, 256), 0)
    lane = lax.broadcasted_iota(jnp.int32, (256, 256), 1)
    keep = lax.rem(row, 4) == lane // 64

    def body(g, carry):
        tile = rows[:, pl.ds(pl.multiple_of(g * 256, 256), 256)]
        wide = jnp.dot(spread[...], tile, preferred_element_type=F32)
        out[g] = jnp.where(keep, wide, 0.0).astype(BF16)
        return carry

    lax.fori_loop(0, 32, body, 0)


def gate_kernel(pair, gain, bias, weight, out):
    def body(n, carry):
        i, j = n // 2, pl.multiple_of(lax.rem(n, 2) * 256, 256)
        values = pair[i, pl.ds(j, 256), :].astype(F32)
        normed = layer_norm(values, gain[...], bias[...]).astype(BF16)
        proj = jnp.dot(normed, weight[...], preferred_element_type=F32)
        out[i, pl.ds(j, 256), :] = sigmoid(proj).astype(BF16)
        return carry

    lax.fori_loop(0, pair.shape[0] * 2, body, 0)


def update_kernel(tiles, n_src, has_out, *refs):
    joff = refs[0]
    sources = refs[1 : 1 + n_src]
    gate, lbd, wide_out, gain, bias = refs[1 + n_src : 6 + n_src]
    refs = refs[6 + n_src + has_out :]
    out, right, product, gates, results, gate_sem, out_sem = refs

    def gate_copy(t, b):
        start = pl.multiple_of(joff[t * 8 + b], 16)
        return pltpu.make_async_copy(
            gate.at[:, pl.ds(start, 16), :], gates.at[t, :, pl.ds(b * 16, 16), :], gate_sem.at[t, b]
        )

    def out_copy(t, b):
        start = pl.multiple_of(joff[t * 8 + b], 16)
        return pltpu.make_async_copy(
            results.at[t, :, pl.ds(b * 16, 16), :], out.at[:, pl.ds(start, 16), :], out_sem.at[t, b]
        )

    for t, tile in enumerate(tiles):
        for b in range(len(tile)):
            gate_copy(t, b).start()
    member = lax.broadcasted_iota(jnp.int32, (8, 128), 0)

    def over_four(total):
        swapped = jnp.where(lax.rem(member, 2) == 0, pltpu.roll(total, 7, 0), pltpu.roll(total, 1, 0))
        total = total + swapped
        swapped = jnp.where(lax.rem(member, 4) < 2, pltpu.roll(total, 6, 0), pltpu.roll(total, 2, 0))
        return total + swapped

    for t, tile in enumerate(tiles):
        for b in range(8):
            for half, (src, row, lane) in enumerate(tile[min(b, len(tile) - 1)]):
                right[b * 16 : b * 16 + 16, half * 4096 : half * 4096 + 4096] = sources[src][
                    row : row + 16, lane : lane + 4096
                ]

        def multiply(g, carry):
            panel = right[:, pl.ds(pl.multiple_of(g * 256, 256), 256)]
            made = lax.dot_general(
                lbd[g], panel, (((1,), (1,)), ((), ())), preferred_element_type=F32
            )
            product[:, g] = made.reshape(32, 8, 128)
            return carry

        lax.fori_loop(0, 32, multiply, 0, unroll=2)
        for b in range(len(tile)):
            gate_copy(t, b).wait()

        def finish(ip, carry):
            values = product[ip]
            mean = over_four(jnp.sum(values, axis=0)) * (1.0 / 128)
            centered = values - mean[None]
            var = over_four(jnp.sum(centered * centered, axis=0)) * (1.0 / 128)
            normed = centered * lax.rsqrt(var + 1e-05)[None] * gain[...] + bias[...]
            normed = normed.reshape(256, 128).astype(BF16)
            both = lax.dot_general(
                normed, wide_out[...], (((0,), (0,)), ((), ())), preferred_element_type=F32
            )
            for i2 in range(2):
                row = 2 * ip + i2
                results[t, row] = (
                    both[:, i2 * 128 : (i2 + 1) * 128] * gates[t, row].astype(F32)
                ).astype(BF16)
            return carry

        lax.fori_loop(0, 32, finish, 0, unroll=2)
        for b in range(len(tile)):
            out_copy(t, b).start()
    for t, tile in enumerate(tiles):
        for b in range(len(tile)):
            out_copy(t, b).wait()


VMEM = pl.BlockSpec(memory_space=pltpu.VMEM)
SMEM = pl.BlockSpec(memory_space=pltpu.SMEM)
ANY = pl.BlockSpec(memory_space=pl.ANY)


def run_update(tiles, joff, sources, gate, lbd, wide_out, gain, bias, before):
    n = len(tiles)
    has_out = before is not None
    args = [joff, *sources, gate, lbd, wide_out, gain, bias] + ([before] if has_out else [])
    specs = [SMEM] + [VMEM] * len(sources) + [ANY, VMEM, VMEM, VMEM, VMEM] + [ANY] * has_out
    shape = gate.shape
    return pl.pallas_call(
        functools.partial(update_kernel, tiles, len(sources), has_out),
        out_shape=jax.ShapeDtypeStruct(shape, BF16),
        in_specs=specs,
        out_specs=ANY,
        scratch_shapes=[
            pltpu.VMEM((128, 8192), BF16),
            pltpu.VMEM((32, 32, 8, 128), F32),
            pltpu.VMEM((n, 64, 128, 128), BF16),
            pltpu.VMEM((n, 64, 128, 128), BF16),
            pltpu.SemaphoreType.DMA((n, 8)),
            pltpu.SemaphoreType.DMA((n, 8)),
        ],
        input_output_aliases={len(args) - 1: 0} if has_out else {},
        compiler_params=pltpu.CompilerParams(vmem_limit_bytes=48 * MIB),
        cost_estimate=pl.CostEstimate(
            flops=n * 3 * 10**9, bytes_accessed=n * 6 * MIB, transcendentals=0
        ),
    )(*args)


def run_right(z, pieces, gain, bias, weight):
    return pl.pallas_call(
        right_kernel,
        out_shape=[jax.ShapeDtypeStruct((16, 4096), BF16)] * 2,
        in_specs=[SMEM] + [VMEM] * 7,
        out_specs=[VMEM] * 2,
        scratch_shapes=[pltpu.VMEM((16, 64, 128), BF16), pltpu.VMEM((64, 16, 128), F32)],
        compiler_params=pltpu.CompilerParams(vmem_limit_bytes=16 * MIB),
    )(z.reshape(1), *pieces, gain, bias, weight)


def run_left(left, gain, bias, weight):
    spread = np.zeros((256, 64), np.float32)
    spread[np.arange(256), np.arange(256) // 4] = 1
    return pl.pallas_call(
        left_kernel,
        out_shape=jax.ShapeDtypeStruct((32, 256, 256), BF16),
        in_specs=[VMEM] * 5,
        out_specs=VMEM,
        scratch_shapes=[
            pltpu.VMEM((16, 64, 128), BF16),
            pltpu.VMEM((64, 16, 128), F32),
            pltpu.VMEM((64, 8192), BF16),
        ],
        compiler_params=pltpu.CompilerParams(vmem_limit_bytes=24 * MIB),
        cost_estimate=pl.CostEstimate(flops=4 * 10**9, bytes_accessed=5 * MIB, transcendentals=0),
    )(left, gain, bias, weight, jnp.asarray(spread, BF16))


def run_gate(pair, gain, bias, weight):
    rows = 8
    block = pl.BlockSpec((rows, 512, 128), lambda n: (n, 0, 0))
    whole = pl.BlockSpec((1, 128), lambda n: (0, 0))
    return pl.pallas_call(
        gate_kernel,
        out_shape=jax.ShapeDtypeStruct(pair.shape, BF16),
        grid=(pair.shape[0] // rows,),
        in_specs=[block, whole, whole, pl.BlockSpec((128, 128), lambda n: (0, 0))],
        out_specs=block,
        compiler_params=pltpu.CompilerParams(vmem_limit_bytes=16 * MIB),
        cost_estimate=pl.CostEstimate(flops=10**10, bytes_accessed=16 * MIB, transcendentals=0),
    )(pair, gain, bias, weight)


def place_a(z, y, x):
    if z == 0:
        if x == 0:
            return "GA", y * 16, 0
        return ("GA", 64, 0) if y == 0 else ("X", (y - 1) * 16, 0)
    if z in (1, 3):
        if x == 0 or y == 0:
            return f"A{z}", 64 if x else y * 16, 0
        return f"PA{z}", (y - 1) * 16, 0
    if x == 0:
        return ("PA1", 48 + y * 16, 0) if y < 3 else ("PA3", 48, 0)
    if y == 0:
        return "PA3", 64, 0
    return ("QA1", (y - 1) * 16, 0) if y < 3 else ("QA3", 0, 0)


def place_b(z, y, x):
    if y == 0:
        if x == 0:
            return "GB", z * 16, 0
        return ("GB", 64, 0) if z == 0 else ("X", (z - 1) * 16, 4096)
    if y in (1, 3):
        if x == 0 or z == 0:
            return f"B{y}", 64 if x else z * 16, 0
        return f"PB{y}", (z - 1) * 16, 0
    if x == 0:
        return ("PB1", 48 + z * 16, 0) if z < 3 else ("PB3", 48, 0)
    if z == 0:
        return "PB3", 64, 0
    return ("QB1", 0, 0) if z == 1 else ("QB3", (z - 2) * 16, 0)


LATE = [(2, 1, 1), (2, 2, 1), (2, 3, 1), (1, 2, 1), (3, 2, 1)]
EARLY = [(z, y, 0) for z in (0, 1, 3) for y in (0, 1, 3)][:8]
OTHERS = [
    (z, y, x)
    for x in range(2)
    for z in range(4)
    for y in range(4)
    if (z, y, x) not in LATE and (z, y, x) not in EARLY
]


def per_device(
    pair_block, left_panel, right_panel, ln_gain, ln_bias, w_left, w_right, w_gate, out_gain, out_bias, w_out
):
    row = lax.axis_index("row")
    z, y, x = row // 8, (row // 2) % 4, row % 2
    c = lax.axis_index("col")
    gain, bias = ln_gain.reshape(1, 128), ln_bias.reshape(1, 128)

    pieces = []
    for s in range(4):
        pairs = [(device_id(z_, y_, x_, c_), device_id(c_ + s, y_, x_, z_)) for z_, y_, x_, c_ in DEVICES]
        part = lax.dynamic_slice_in_dim(right_panel, ((c + s) % 4) * 16, 16, 0)
        pieces.append(lax.ppermute(part, AXES, pairs))
    left_all = lax.all_gather(left_panel, "col", axis=0, tiled=False)
    a, b = run_right(z.astype(jnp.int32), pieces, gain, bias, w_right)

    def cat(*parts):
        return jnp.concatenate(parts, 0)

    got = {}
    xab = move(jnp.concatenate([a, b], 1), dx=1)
    got["GA"] = cat(a, move(a, dy=-1), move(a, dy=2), move(a, dy=1), xab[:, :4096])
    got["GB"] = cat(b, move(b, dz=-1), move(b, dz=2), move(b, dz=1), xab[:, 4096:])
    got["A1"], got["A3"] = move(got["GA"], dz=-1), move(got["GA"], dz=1)
    got["B1"], got["B3"] = move(got["GB"], dy=-1), move(got["GB"], dy=1)
    other = move(jnp.concatenate([got["GA"][16:64], got["GB"][16:64]], 1), dx=1)
    got["X"] = other
    got["PA1"] = move(cat(other[:, :4096], got["A1"][:48]), dz=-1)
    got["PA3"] = move(cat(other[:, :4096], got["A3"][48:]), dz=1)
    got["PB1"] = move(cat(other[:, 4096:], got["B1"][:48]), dy=-1)
    got["PB3"] = move(cat(other[:, 4096:], got["B3"][48:]), dy=1)
    got["QA1"], got["QA3"] = move(got["PA1"][:32], dz=-1), move(got["PA3"][32:48], dz=1)
    got["QB1"], got["QB3"] = move(got["PB1"][:16], dy=-1), move(got["PB3"][16:48], dy=1)

    lbd = run_left(left_all, gain, bias, w_left)
    gate = run_gate(pair_block, gain, bias, w_gate)

    order = hidden_order()
    perm_out = w_out[order].reshape(32, 1, 4, 128)
    eye = jnp.eye(2, dtype=BF16)
    wide_out = (perm_out[:, :, :, None, :] * eye[None, :, None, :, None]).reshape(256, 256)

    def spread(vector):
        rows = jnp.broadcast_to(vector[order].reshape(32, 1, 4), (32, 2, 4)).reshape(32, 8, 1)
        return jnp.broadcast_to(rows, (32, 8, 128))

    gain_out, bias_out = spread(out_gain), spread(out_bias)

    def call(blocks, before):
        names = sorted({p(*d)[0] for d in blocks for p in (place_a, place_b)})
        tiles, joff = [], []
        for at in range(0, len(blocks), 8):
            tile = blocks[at : at + 8]
            tiles.append(
                [
                    tuple((names.index(p(*d)[0]), p(*d)[1], p(*d)[2]) for p in (place_a, place_b))
                    for d in tile
                ]
            )
            for dz, dy, dx in tile + [tile[0]] * (8 - len(tile)):
                joff.append((((y + dy) % 4) * 2 + (x + dx) % 2) * 64 + ((z + dz) % 4) * 16)
        return run_update(
            tiles,
            jnp.stack(joff).astype(jnp.int32),
            [got[n] for n in names],
            gate,
            lbd,
            wide_out,
            gain_out,
            bias_out,
            before,
        )

    out = call(EARLY, None)
    out = call(OTHERS[:16], out)
    return call(LATE + OTHERS[16:], out)


def solution(mesh):
    part = P("row", "col", None)
    in_specs = (part, part, part) + (P(),) * 8
    return jax.shard_map(per_device, mesh=mesh, in_specs=in_specs, out_specs=part, check_vma=False)
```

```python
import functools

import jax
import jax.numpy as jnp
import numpy as np
from jax import lax
from jax.experimental import pallas as pl
from jax.experimental.pallas import tpu as pltpu
from jax.sharding import PartitionSpec as P

AXES = ("row", "col")
BF16, F32 = jnp.bfloat16, jnp.float32
DEVICES = [(z, y, x, c) for z in range(4) for y in range(4) for x in range(2) for c in range(4)]
MIB = 1 << 20


def device_id(z, y, x, c):
    return (((z % 4) * 4 + y % 4) * 2 + x % 2) * 4 + c


def move(value, dz=0, dy=0, dx=0, dc=0):
    pairs = [
        (device_id(z, y, x, c), device_id(z + dz, y + dy, x + dx, c ^ dc)) for z, y, x, c in DEVICES
    ]
    return lax.ppermute(value, AXES, pairs)


def sigmoid(values):
    return 0.5 * jnp.tanh(0.5 * values) + 0.5


def hidden_order():
    order = []
    for group in range(32):
        first = 2 * group
        order += [first, first + 64, first + 1, first + 65]
    return np.array(order)


def norm_rows(values, average, gain, bias):
    mean = jnp.dot(values, average, preferred_element_type=F32)
    centered = values.astype(F32) - mean
    var = jnp.dot((centered * centered).astype(BF16), average, preferred_element_type=F32)
    return (centered * lax.rsqrt(var + 1e-05) * gain.reshape(1, 128) + bias.reshape(1, 128)).astype(BF16)


def project_16(normed, weight, swap, store):
    proj = lax.dot_general(
        weight, normed.reshape(16 * 64, 128), (((0,), (1,)), ((), ())), preferred_element_type=F32
    )
    value = (sigmoid(proj[:128]) * proj[128:]).astype(BF16).astype(F32)
    low, high = value[:64], value[64:]
    lane = lax.broadcasted_iota(jnp.int32, (64, 128), 1)
    for pair in range(8):
        lo = low[:, pair * 128 : (pair + 1) * 128]
        hi = high[:, pair * 128 : (pair + 1) * 128]
        swap[:, 2 * pair, :] = jnp.where(lane < 64, lo, pltpu.roll(hi, 64, 1))
        swap[:, 2 * pair + 1, :] = jnp.where(lane < 64, pltpu.roll(lo, 64, 1), hi)
    for h in range(64):
        store(h, swap[h].astype(BF16))


def right_kernel(here, p0, p1, p2, p3, gain_in, bias_in, weight_in, out, normed, swap, gain, bias, weight, sem):
    fetches = [
        pltpu.make_async_copy(source, target, sem.at[n])
        for n, (source, target) in enumerate(((gain_in, gain), (bias_in, bias), (weight_in, weight)))
    ]
    for fetch in fetches:
        fetch.start()
    for fetch in fetches:
        fetch.wait()
    average = jnp.full((128, 128), 1 / 128, BF16)
    for s, piece in enumerate((p0, p1, p2, p3)):
        start = pl.multiple_of(lax.rem(here[0] - s + 4, 4) * 16, 16)
        made = norm_rows(piece[...].reshape(256, 128), average, gain[...], bias[...])
        normed[:, pl.ds(start, 16), :] = made.reshape(16, 16, 128)

    def store(h, tile):
        out[:, h * 128 : (h + 1) * 128] = tile

    project_16(normed[...], weight[...], swap, store)


def left_kernel(
    here, left_0, left_1, average, gain, bias, weight, spread, order, w_out, out_gain, out_bias,
    out, wide_out, wide_gain, wide_bias, normed, swap, rows,
):
    for quarter in range(4):
        at = slice(quarter * 16, quarter * 16 + 16)
        mine = normed.at[quarter]
        for flip in range(4):
            piece = (left_0, left_1)[flip % 2][flip // 2, at].reshape(256, 128)
            start = pl.multiple_of((here[3] ^ flip) * 16, 16)
            made = norm_rows(piece, average[...], gain[...], bias[...])
            mine[:, pl.ds(start, 16), :] = made.reshape(16, 16, 128)

        def store(h, tile, at=at):
            rows[at, h * 128 : (h + 1) * 128] = tile

        project_16(mine[...], weight[...], swap.at[quarter], store)
    row = lax.broadcasted_iota(jnp.int32, (256, 256), 0)
    lane = lax.broadcasted_iota(jnp.int32, (256, 256), 1)
    keep = lax.rem(row, 4) == lane // 64

    def body(g, carry):
        tile = rows[:, pl.ds(pl.multiple_of(g * 256, 256), 256)]
        wide = jnp.dot(spread[...], tile, preferred_element_type=F32)
        out[g] = jnp.where(keep, wide, 0.0).astype(BF16)
        return carry

    lax.fori_loop(0, 32, body, 0, unroll=32)
    made = jnp.dot(order[...], w_out[...].astype(F32), preferred_element_type=F32)
    second = lax.rem(lax.broadcasted_iota(jnp.int32, (256, 128), 0), 8) // 4
    wide_out[:, :128] = jnp.where(second == 0, made, 0.0).astype(BF16)
    wide_out[:, 128:] = jnp.where(second == 1, made, 0.0).astype(BF16)
    for source, target in ((out_gain, wide_gain), (out_bias, wide_bias)):
        columns = jnp.broadcast_to(source[...], (128, 128)).T
        made = jnp.dot(
            order[...], columns, preferred_element_type=F32, precision=lax.Precision.HIGHEST
        )
        target[...] = made.reshape(32, 8, 128)


def gate_block(average, weight, bias, pair, out):
    for i in range(0, pair.shape[0], 2):
        both = jnp.concatenate([pair[i], pair[i + 1]], 1)
        mean = jnp.dot(both, average[...], preferred_element_type=F32)
        centered = (both.astype(F32) - mean).astype(BF16)
        var = jnp.dot(centered * centered, average[...], preferred_element_type=F32)
        proj = jnp.dot(centered, weight[...], preferred_element_type=F32)
        proj = proj * lax.rsqrt(var + 1e-05) + bias[...]
        gate = (0.5 * jnp.tanh(proj) + 0.5).astype(BF16)
        out[i], out[i + 1] = gate[:, :128], gate[:, 128:]


def gate_kernel(half, pair, average, weight, bias, out):
    rows, first = 8, half * 4
    pltpu.emit_pipeline(
        functools.partial(gate_block, average, weight, bias),
        grid=(4,),
        in_specs=[pl.BlockSpec((rows, 512, 128), lambda n: (n + first, 0, 0))],
        out_specs=[pl.BlockSpec((rows, 512, 128), lambda n: (n, 0, 0))],
    )(pair, out)


def update_kernel(blocks, n_src, has_out, *refs):
    here = refs[0]
    sources = refs[1 : 1 + n_src]
    gate_0, gate_1, lbd, wide_out, gain, bias = refs[1 + n_src : 7 + n_src]
    refs = refs[7 + n_src + has_out :]
    out, right, product, gates, results, gate_sem, out_sem = refs
    z, y, x = here[0], here[1], here[2]
    columns = 16 * len(blocks)

    def column(b):
        dz, dy, dx = blocks[b][0]
        start = (lax.rem(y + dy, 4) * 2 + lax.rem(x + dx, 2)) * 64 + lax.rem(z + dz, 4) * 16
        return pl.ds(pl.multiple_of(start, 16), 16)

    def gate_copy(b, half):
        return pltpu.make_async_copy(
            (gate_0, gate_1)[half].at[:, column(b), :],
            gates.at[pl.ds(half * 32, 32), pl.ds(b * 16, 16), :],
            gate_sem.at[b, half],
        )

    def out_copy(b, q):
        rows = pl.ds(q * 16, 16)
        return pltpu.make_async_copy(
            results.at[rows, pl.ds(b * 16, 16), :], out.at[rows, column(b), :], out_sem.at[b, q]
        )

    for b in range(len(blocks)):
        gate_copy(b, 0).start()
        gate_copy(b, 1).start()
    member = lax.broadcasted_iota(jnp.int32, (8, 128), 0)

    def over_four(total):
        swapped = jnp.where(lax.rem(member, 2) == 0, pltpu.roll(total, 7, 0), pltpu.roll(total, 1, 0))
        total = total + swapped
        swapped = jnp.where(lax.rem(member, 4) < 2, pltpu.roll(total, 6, 0), pltpu.roll(total, 2, 0))
        return total + swapped

    for b, (_, halves) in enumerate(blocks):
        for half, (src, row, lane) in enumerate(halves):
            right[b * 16 : b * 16 + 16, half * 4096 : half * 4096 + 4096] = sources[src][
                row : row + 16, lane : lane + 4096
            ]

    def multiply(g, carry):
        panel = right[:, pl.ds(pl.multiple_of(g * 256, 256), 256)]
        made = lax.dot_general(lbd[g], panel, (((1,), (1,)), ((), ())), preferred_element_type=F32)
        product[:, g] = made.reshape(32, 8, columns)
        return carry

    lax.fori_loop(0, 32, multiply, 0, unroll=16)
    for b in range(len(blocks)):
        gate_copy(b, 0).wait()
        gate_copy(b, 1).wait()

    def finish(ip, carry):
        for part in range(columns // 128):
            lanes = slice(part * 128, part * 128 + 128)
            values = product[ip, :, :, lanes]
            mean = over_four(jnp.sum(values, axis=0)) * (1.0 / 128)
            centered = values - mean[None]
            var = over_four(jnp.sum(centered * centered, axis=0)) * (1.0 / 128)
            normed = centered * lax.rsqrt(var + 1e-05)[None] * gain[...] + bias[...]
            normed = normed.reshape(256, 128).astype(BF16)
            both = lax.dot_general(
                normed, wide_out[...], (((0,), (0,)), ((), ())), preferred_element_type=F32
            )
            for i2 in range(2):
                row = 2 * ip + i2
                gate = gates[row, lanes].astype(F32)
                results[row, lanes] = (both[:, i2 * 128 : (i2 + 1) * 128] * gate).astype(BF16)
        return carry

    for q in range(4):
        lax.fori_loop(q * 8, q * 8 + 8, finish, 0, unroll=8 * 128 // columns)
        for b in range(len(blocks)):
            out_copy(b, q).start()
    for b in range(len(blocks)):
        for q in range(4):
            out_copy(b, q).wait()


VMEM = pl.BlockSpec(memory_space=pltpu.VMEM)
SMEM = pl.BlockSpec(memory_space=pltpu.SMEM)
HBM = pl.BlockSpec(memory_space=pltpu.HBM)


def run_update(blocks, here, sources, gates, lbd, wide_out, gain, bias, before):
    n = len(blocks)
    has_out = before is not None
    args = [here, *sources, *gates, lbd, wide_out, gain, bias] + ([before] if has_out else [])
    return pl.pallas_call(
        functools.partial(update_kernel, blocks, len(sources), has_out),
        out_shape=pltpu.HBM((64, 512, 128), BF16),
        in_specs=[SMEM] + [VMEM] * len(sources) + [HBM] * 2 + [VMEM] * 4 + [HBM] * has_out,
        out_specs=HBM,
        scratch_shapes=[
            pltpu.VMEM((n * 16, 8192), BF16),
            pltpu.VMEM((32, 32, 8, n * 16), F32),
            pltpu.VMEM((64, n * 16, 128), BF16),
            pltpu.VMEM((64, n * 16, 128), BF16),
            pltpu.SemaphoreType.DMA((n, 2)),
            pltpu.SemaphoreType.DMA((n, 4)),
        ],
        input_output_aliases={len(args) - 1: 0} if has_out else {},
        compiler_params=pltpu.CompilerParams(vmem_limit_bytes=(8 + 3 * n // 2) * MIB),
        cost_estimate=pl.CostEstimate(flops=n * 4 * 10**8, bytes_accessed=n * MIB, transcendentals=0),
    )(*args)


def run_right(here, pieces, *weights):
    weights = [pltpu.with_memory_space_constraint(w, pltpu.HBM) for w in weights]
    return pl.pallas_call(
        right_kernel,
        out_shape=jax.ShapeDtypeStruct((16, 8192), BF16),
        in_specs=[SMEM] + [VMEM] * 4 + [HBM] * 3,
        out_specs=VMEM,
        scratch_shapes=[
            pltpu.VMEM((16, 64, 128), BF16),
            pltpu.VMEM((64, 16, 128), F32),
            pltpu.VMEM((128,), F32),
            pltpu.VMEM((128,), F32),
            pltpu.VMEM((128, 256), BF16),
            pltpu.SemaphoreType.DMA((3,)),
        ],
        compiler_params=pltpu.CompilerParams(vmem_limit_bytes=16 * MIB),
    )(here, *pieces, *weights)


def run_left(here, left_0, left_1, gain, bias, weight, w_out, out_gain, out_bias):
    spread = np.zeros((256, 64), np.float32)
    spread[np.arange(256), np.arange(256) // 4] = 1
    order = np.zeros((32, 2, 4, 128), np.float32)
    for n, h in enumerate(hidden_order()):
        order[n // 4, :, n % 4, h] = 1
    return pl.pallas_call(
        left_kernel,
        out_shape=[
            jax.ShapeDtypeStruct((32, 256, 256), BF16),
            jax.ShapeDtypeStruct((256, 256), BF16),
            jax.ShapeDtypeStruct((32, 8, 128), F32),
            jax.ShapeDtypeStruct((32, 8, 128), F32),
        ],
        in_specs=[SMEM] + [VMEM] * 11,
        out_specs=[VMEM] * 4,
        scratch_shapes=[
            pltpu.VMEM((4, 16, 64, 128), BF16),
            pltpu.VMEM((4, 64, 16, 128), F32),
            pltpu.VMEM((64, 8192), BF16),
        ],
        compiler_params=pltpu.CompilerParams(vmem_limit_bytes=20 * MIB),
        cost_estimate=pl.CostEstimate(flops=4 * 10**9, bytes_accessed=12 * MIB, transcendentals=0),
    )(
        here, left_0, left_1, jnp.full((128, 128), 1 / 128, BF16), gain, bias, weight, jnp.asarray(spread, BF16), jnp.asarray(order.reshape(256, 128)),
        w_out, out_gain.reshape(1, 128), out_bias.reshape(1, 128),
    )


def gate_weights(gain, bias, weight):
    eye = jnp.eye(2, dtype=F32)
    weight = weight.astype(F32)
    wide = jnp.kron(eye, gain.reshape(128, 1) * weight * 0.5).astype(BF16)
    shift = 0.5 * jnp.dot(bias, weight, precision=lax.Precision.HIGHEST)
    return wide, jnp.tile(shift, (1, 2))


def run_gate(half, pair, wide, shift):
    average = jnp.kron(jnp.eye(2, dtype=BF16), jnp.full((128, 128), 1 / 128, BF16))
    return pl.pallas_call(
        functools.partial(gate_kernel, half),
        out_shape=pltpu.HBM((32, 512, 128), BF16),
        in_specs=[HBM, VMEM, VMEM, VMEM],
        out_specs=HBM,
        compiler_params=pltpu.CompilerParams(vmem_limit_bytes=20 * MIB),
        cost_estimate=pl.CostEstimate(flops=8 * 10**9, bytes_accessed=1 * MIB, transcendentals=0),
    )(pltpu.with_memory_space_constraint(pair, pltpu.HBM), average, wide, shift)


def place(near, far, x, own, first, other):
    if x == 0:
        if near == 0 or far == 0:
            return own(near, far), 0
        if far != 2:
            return f"{first}{far}", (near - 1) * 16
        return (f"P{first}1", 16 + near * 16) if near < 3 else (f"P{first}3", 32)
    if far == 0:
        if near == 0:
            return "X0", 0
        return (f"{other}1", 64) if near == 1 else ("X2", (near - 2) * 16)
    if far != 2:
        if near == 0:
            return f"{first}{far}", 48
        if near == 2:
            return "X3", 0 if far == 1 else 16
        return f"P{first}{far}", 0 if near == 1 else 16
    if near == 0:
        return f"P{first}3", 48
    return (f"Q{first}1", (near - 1) * 16) if near < 3 else (f"Q{first}3", 0)


def place_a(z, y, x):
    own = lambda near, far: f"Z{far}" if near == 0 and far else f"Y{near}"
    name, row = place(y, z, x, own, "A", "B")
    return name, row, 0


def place_b(z, y, x):
    own = lambda near, far: f"Y{far}" if near == 0 and far else (f"Z{near}" if near else "Y0")
    name, row = place(z, y, x, own, "B", "A")
    return name, row, 4096 if name[0] in "XYZ" else 0


EARLY = [(z, y, 0) for z in (0, 1, 3) for y in (0, 1, 3)] + [(2, 0, 0), (0, 2, 0)]
EARLY += [(0, 0, 1), (1, 0, 1), (3, 0, 1), (0, 1, 1), (0, 3, 1)]
LATE = [(2, 1, 1), (2, 2, 1), (2, 3, 1), (1, 2, 1), (3, 2, 1)]
OTHERS = [
    (z, y, x)
    for x in range(2)
    for z in range(4)
    for y in range(4)
    if (z, y, x) not in LATE and (z, y, x) not in EARLY
]


def per_device(
    pair_block, left_panel, right_panel, ln_gain, ln_bias, w_left, w_right, w_gate, out_gain, out_bias, w_out
):
    row = lax.axis_index("row")
    z, y, x = row // 8, (row // 2) % 4, row % 2
    c = lax.axis_index("col")
    gain, bias = ln_gain.reshape(1, 128), ln_bias.reshape(1, 128)

    here = jnp.stack([z, y, x, c]).astype(jnp.int32)

    pieces = []
    for s in range(4):
        pairs = [(device_id(z_, y_, x_, c_), device_id(c_ + s, y_, x_, z_)) for z_, y_, x_, c_ in DEVICES]
        part = lax.dynamic_slice_in_dim(right_panel, ((c + s) % 4) * 16, 16, 0)
        pieces.append(lax.ppermute(part, AXES, pairs))
    rows = run_right(here, pieces, ln_gain, ln_bias, w_right)
    left_2 = move(left_panel, dc=2)
    rows, left_2, wide_gate = lax.optimization_barrier(
        (rows, left_2, gate_weights(ln_gain, ln_bias, w_gate))
    )

    def cat(*parts):
        return jnp.concatenate(parts, 0)

    got = {}
    def together(*names, more=()):
        held = lax.optimization_barrier([got[n] for n in names] + list(more))
        got.update(zip(names, held))
        return held[len(names) :]

    def call(blocks, before):
        names = sorted({p(*d)[0] for d in blocks for p in (place_a, place_b)})
        found = []
        for d in blocks:
            places = [p(*d) for p in (place_a, place_b)]
            found.append((d, [(names.index(name), row, lane) for name, row, lane in places]))
        sources = [got[n] for n in names]
        return run_update(found, here, sources, gates, lbd, wide_out, gain_out, bias_out, before)

    def halves(a, b):
        return jnp.concatenate([a, b], 1)

    got["Y0"] = rows
    got["X0"] = move(rows, dx=1)
    for step in (1, 3):
        got[f"Y{step}"], got[f"Z{step}"] = move(rows, dy=-step), move(rows, dz=-step)
    got["X0"], again = lax.optimization_barrier((got["X0"], rows))
    got["Y2"] = move(again, dy=2)
    got["Y1"], again = lax.optimization_barrier((got["Y1"], again))
    got["Z2"] = move(again, dz=2)
    gate_0 = run_gate(0, pair_block, *wide_gate)
    ones = ("Y1", "Y2", "Y3", "Z1", "Z2", "Z3", "X0")
    gate_0, left_2 = together(*ones, more=[gate_0, left_2])
    half_a = [got[n][:, :4096] for n in ones]
    half_b = [got[n][:, 4096:] for n in ones]
    to_z, to_y = cat(*half_a[:3], half_a[6]), cat(*half_b[3:])
    got["A1"], got["A3"] = move(cat(to_z, half_b[6]), dz=-1), move(to_z, dz=1)
    got["B1"], got["B3"] = move(cat(to_y, half_a[6]), dy=-1), move(to_y, dy=1)
    got["X2"] = move(halves(cat(*half_a[1:3]), cat(*half_b[4:6])), dx=1)
    left_0 = jnp.stack([left_panel, left_2])
    left_1 = move(left_0, dc=1)
    gate_1 = run_gate(1, pair_block, *wide_gate)
    lbd, wide_out, gain_out, bias_out = run_left(
        here, left_0, left_1, gain, bias, w_left, w_out, out_gain, out_bias
    )
    gate_1, lbd = together("A1", "A3", "B1", "B3", "X2", more=[gate_1, lbd])
    gates = (gate_0, gate_1)
    a1, a3, b1, b3, x2 = (got[n] for n in ("A1", "A3", "B1", "B3", "X2"))
    xa, xb = cat(b1[64:], x2[16:, :4096]), cat(a1[64:], x2[16:, 4096:])
    got["PA1"], got["PA3"] = move(cat(xa, a1[:32]), dz=-1), move(cat(xa, a3[32:]), dz=1)
    got["PB1"], got["PB3"] = move(cat(xb, b1[:32]), dy=-1), move(cat(xb, b3[32:]), dy=1)
    got["X3"] = move(halves(cat(a1[16:32], a3[16:32]), cat(b1[16:32], b3[16:32])), dx=1)
    out = call(EARLY, None)
    (out,) = together("PA1", "PA3", "PB1", "PB3", "X3", more=[out])
    x3 = got["X3"]
    got["QA1"], got["QA3"] = move(cat(got["PA1"][:16], x3[:16, :4096]), dz=-1), move(got["PA3"][16:32], dz=1)
    got["QB1"], got["QB3"] = move(cat(got["PB1"][:16], x3[:16, 4096:]), dy=-1), move(got["PB3"][16:32], dy=1)
    out = call(OTHERS[:8], out)
    (out,) = together("QA1", "QA3", "QB1", "QB3", more=[out])
    return call(LATE + OTHERS[8:], out)


def solution(mesh):
    part = P("row", "col", None)
    in_specs = (part, part, part) + (P(),) * 8
    return jax.shard_map(per_device, mesh=mesh, in_specs=in_specs, out_specs=part, check_vma=False)
```

```python
import functools

import jax
import jax.numpy as jnp
import numpy as np
from jax import lax
from jax.experimental import pallas as pl
from jax.experimental.pallas import tpu as pltpu
from jax.sharding import PartitionSpec as P

AXES = ("row", "col")
BF16, F32 = jnp.bfloat16, jnp.float32
DEVICES = [(z, y, x, c) for z in range(4) for y in range(4) for x in range(2) for c in range(4)]
MIB = 1 << 20
PARTS = 4
GATE_FIRST = 16


def device_id(z, y, x, c):
    return (((z % 4) * 4 + y % 4) * 2 + x % 2) * 4 + c


def move(value, dz=0, dy=0, dx=0, dc=0):
    pairs = [
        (device_id(z, y, x, c), device_id(z + dz, y + dy, x + dx, c ^ dc)) for z, y, x, c in DEVICES
    ]
    return lax.ppermute(value, AXES, pairs)


def sigmoid(values):
    return 0.5 * jnp.tanh(0.5 * values) + 0.5


def hidden_order():
    order = []
    for group in range(32):
        first = 2 * group
        order += [first, first + 64, first + 1, first + 65]
    return np.array(order)


def standardize(values, average):
    mean = jnp.dot(values, average, preferred_element_type=F32)
    centered = values.astype(F32) - mean
    var = jnp.dot((centered * centered).astype(BF16), average, preferred_element_type=F32)
    return centered * lax.rsqrt(var + 1e-05)


def scale(values, gain, bias):
    return (values * gain.reshape(1, 128) + bias.reshape(1, 128)).astype(BF16)


def project_16(normed, weight, swap, store):
    proj = lax.dot_general(
        weight, normed.reshape(16 * 64, 128), (((0,), (1,)), ((), ())), preferred_element_type=F32
    )
    value = (sigmoid(proj[:128]) * proj[128:]).astype(BF16).astype(F32)
    low, high = value[:64], value[64:]
    lane = lax.broadcasted_iota(jnp.int32, (64, 128), 1)
    for pair in range(8):
        lo = low[:, pair * 128 : (pair + 1) * 128]
        hi = high[:, pair * 128 : (pair + 1) * 128]
        swap[:, 2 * pair, :] = jnp.where(lane < 64, lo, pltpu.roll(hi, 64, 1))
        swap[:, 2 * pair + 1, :] = jnp.where(lane < 64, pltpu.roll(lo, 64, 1), hi)
    for h in range(64):
        store(h, swap[h].astype(BF16))


def prepare_kernel(gain_in, bias_in, right_in, gate_in, gain, bias, right, wide, shift, gain_row, bias_row, gate, sem):
    pairs = ((gain_in, gain_row), (bias_in, bias_row), (right_in, right), (gate_in, gate))
    fetches = [pltpu.make_async_copy(source, target, sem.at[n]) for n, (source, target) in enumerate(pairs)]
    for fetch in fetches:
        fetch.start()
    for fetch in fetches:
        fetch.wait()
    gain[...] = gain_row[...].reshape(1, 128)
    bias[...] = bias_row[...].reshape(1, 128)
    half = 0.5 * gate[...].astype(F32)
    block = (jnp.broadcast_to(gain[...], (128, 128)).T * half).astype(BF16)
    wide[...] = jnp.zeros((256, 256), BF16)
    wide[:128, :128] = block
    wide[128:, 128:] = block
    rows = jnp.broadcast_to(bias[...], (8, 128))
    made = jnp.dot(rows, half, preferred_element_type=F32, precision=lax.Precision.HIGHEST)[:1]
    shift[:, :128] = made
    shift[:, 128:] = made


def right_kernel(here, p0, p1, p2, p3, gain, bias, weight, out, normed, swap):
    average = jnp.full((128, 128), 1 / 128, BF16)
    for s, piece in enumerate((p0, p1, p2, p3)):
        start = pl.multiple_of(lax.rem(here[0] - s + 4, 4) * 16, 16)
        made = scale(standardize(piece[...].reshape(256, 128), average), gain[...], bias[...])
        normed[:, pl.ds(start, 16), :] = made.reshape(16, 16, 128)

    def store(h, tile):
        out[:, h * 128 : (h + 1) * 128] = tile

    project_16(normed[...], weight[...], swap, store)


def left_kernel(
    here, left_0, left_1, average, gain, bias, weight, spread, order, w_out, out_gain, out_bias,
    out, wide_out, wide_gain, wide_bias, normed, swap, rows,
):
    for quarter in range(4):
        at = slice(quarter * 16, quarter * 16 + 16)
        mine = normed.at[quarter]
        for flip in range(4):
            piece = (left_0, left_1)[flip % 2][flip // 2, at].reshape(256, 128)
            start = pl.multiple_of((here[3] ^ flip) * 16, 16)
            made = scale(standardize(piece, average[...]), gain[...], bias[...])
            mine[:, pl.ds(start, 16), :] = made.reshape(16, 16, 128)

        def store(h, tile, at=at):
            rows[at, h * 128 : (h + 1) * 128] = tile

        project_16(mine[...], weight[...], swap.at[quarter], store)
    row = lax.broadcasted_iota(jnp.int32, (256, 256), 0)
    lane = lax.broadcasted_iota(jnp.int32, (256, 256), 1)
    keep = lax.rem(row, 4) == lane // 64

    def body(g, carry):
        tile = rows[:, pl.ds(pl.multiple_of(g * 256, 256), 256)]
        wide = jnp.dot(spread[...], tile, preferred_element_type=F32)
        out[g] = jnp.where(keep, wide, 0.0).astype(BF16)
        return carry

    lax.fori_loop(0, 32, body, 0, unroll=32)
    made = jnp.dot(order[...], w_out[...].astype(F32), preferred_element_type=F32)
    second = lax.rem(lax.broadcasted_iota(jnp.int32, (256, 128), 0), 8) // 4
    wide_out[:, :128] = jnp.where(second == 0, made, 0.0).astype(BF16)
    wide_out[:, 128:] = jnp.where(second == 1, made, 0.0).astype(BF16)
    for source, target in ((out_gain, wide_gain), (out_bias, wide_bias)):
        columns = jnp.broadcast_to(source[...], (128, 128)).T
        made = jnp.dot(
            order[...], columns, preferred_element_type=F32, precision=lax.Precision.HIGHEST
        )
        target[...] = made.reshape(32, 8, 128)


def gate_block(average, weight, bias, pair, out):
    for i in range(0, pair.shape[0], 2):
        both = jnp.concatenate([pair[i], pair[i + 1]], 1)
        mean = jnp.dot(both, average[...], preferred_element_type=F32)
        centered = (both.astype(F32) - mean).astype(BF16)
        var = jnp.dot(centered * centered, average[...], preferred_element_type=F32)
        proj = jnp.dot(centered, weight[...], preferred_element_type=F32)
        proj = proj * lax.rsqrt(var + 1e-05) + bias[...]
        gate = (0.5 * jnp.tanh(proj) + 0.5).astype(BF16)
        out[i], out[i + 1] = gate[:, :128], gate[:, 128:]


def gate_kernel(first, pair, average, weight, bias, out):
    pltpu.emit_pipeline(
        functools.partial(gate_block, average, weight, bias),
        grid=(out.shape[0] // 16,),
        in_specs=[pl.BlockSpec((16, 512, 128), lambda n: (n + first, 0, 0))],
        out_specs=[pl.BlockSpec((16, 512, 128), lambda n: (n, 0, 0))],
    )(pair, out)


def update_kernel(blocks, n_src, has_out, *refs):
    here = refs[0]
    sources = refs[1 : 1 + n_src]
    gate_0, gate_1, lbd, wide_out, gain, bias = refs[1 + n_src : 7 + n_src]
    refs = refs[7 + n_src + has_out :]
    out, product, gates, results, gate_sem, out_sem = refs
    z, y, x = here[0], here[1], here[2]
    columns = 16 * len(blocks)

    def column(b):
        dz, dy, dx = blocks[b][0]
        start = (lax.rem(y + dy, 4) * 2 + lax.rem(x + dx, 2)) * 64 + lax.rem(z + dz, 4) * 16
        return pl.ds(pl.multiple_of(start, 16), 16)

    def gate_copy(b, half):
        return pltpu.make_async_copy(
            (gate_0, gate_1)[half].at[:, column(b), :],
            gates.at[pl.ds(half * GATE_FIRST, (GATE_FIRST, 64 - GATE_FIRST)[half]), pl.ds(b * 16, 16), :],
            gate_sem.at[b, half],
        )

    def out_copy(b, q):
        rows = pl.ds(q * 64 // PARTS, 64 // PARTS)
        return pltpu.make_async_copy(
            results.at[rows, pl.ds(b * 16, 16), :], out.at[rows, column(b), :], out_sem.at[b, q]
        )

    for b in range(len(blocks)):
        gate_copy(b, 0).start()
        gate_copy(b, 1).start()
    member = lax.broadcasted_iota(jnp.int32, (8, 128), 0)

    def over_four(total):
        swapped = jnp.where(lax.rem(member, 2) == 0, pltpu.roll(total, 7, 0), pltpu.roll(total, 1, 0))
        total = total + swapped
        swapped = jnp.where(lax.rem(member, 4) < 2, pltpu.roll(total, 6, 0), pltpu.roll(total, 2, 0))
        return total + swapped

    for half in range(2):

        def multiply(g, carry, half=half):
            parts = []
            for _, halves in blocks:
                src, row, lane = halves[half]
                at = pl.ds(pl.multiple_of(lane + g * 256, 256), 256)
                parts.append(sources[src][row : row + 16, at])
            made = lax.dot_general(
                lbd[half * 16 + g],
                jnp.concatenate(parts, 0),
                (((1,), (1,)), ((), ())),
                preferred_element_type=F32,
            )
            product[:, half * 16 + g] = made.reshape(32, 8, columns)
            return carry

        lax.fori_loop(0, 16, multiply, 0, unroll=16)
    for b in range(len(blocks)):
        gate_copy(b, 0).wait()
        gate_copy(b, 1).wait()

    def finish(ip, carry):
        for part in range(columns // 128):
            lanes = slice(part * 128, part * 128 + 128)
            values = product[ip, :, :, lanes]
            mean = over_four(jnp.sum(values, axis=0)) * (1.0 / 128)
            centered = values - mean[None]
            var = over_four(jnp.sum(centered * centered, axis=0)) * (1.0 / 128)
            normed = centered * lax.rsqrt(var + 1e-05)[None] * gain[...] + bias[...]
            normed = normed.reshape(256, 128).astype(BF16)
            both = lax.dot_general(
                normed, wide_out[...], (((0,), (0,)), ((), ())), preferred_element_type=F32
            )
            for i2 in range(2):
                row = 2 * ip + i2
                gate = gates[row, lanes].astype(F32)
                results[row, lanes] = (both[:, i2 * 128 : (i2 + 1) * 128] * gate).astype(BF16)
        return carry

    for q in range(PARTS):
        lax.fori_loop(q * 32 // PARTS, (q + 1) * 32 // PARTS, finish, 0, unroll=8)
        for b in range(len(blocks)):
            out_copy(b, q).start()
    for b in range(len(blocks)):
        for q in range(PARTS):
            out_copy(b, q).wait()


VMEM = pl.BlockSpec(memory_space=pltpu.VMEM)
SMEM = pl.BlockSpec(memory_space=pltpu.SMEM)
HBM = pl.BlockSpec(memory_space=pltpu.HBM)


def run_update(blocks, here, sources, gates, lbd, wide_out, gain, bias, before):
    n = len(blocks)
    has_out = before is not None
    args = [here, *sources, *gates, lbd, wide_out, gain, bias] + ([before] if has_out else [])
    return pl.pallas_call(
        functools.partial(update_kernel, blocks, len(sources), has_out),
        out_shape=pltpu.HBM((64, 512, 128), BF16),
        in_specs=[SMEM] + [VMEM] * len(sources) + [HBM] * 2 + [VMEM] * 4 + [HBM] * has_out,
        out_specs=HBM,
        scratch_shapes=[
            pltpu.VMEM((32, 32, 8, n * 16), F32),
            pltpu.VMEM((64, n * 16, 128), BF16),
            pltpu.VMEM((64, n * 16, 128), BF16),
            pltpu.SemaphoreType.DMA((n, 2)),
            pltpu.SemaphoreType.DMA((n, PARTS)),
        ],
        input_output_aliases={len(args) - 1: 0} if has_out else {},
        compiler_params=pltpu.CompilerParams(vmem_limit_bytes=(8 + 5 * n // 4) * MIB),
        cost_estimate=pl.CostEstimate(flops=n * 4 * 10**8, bytes_accessed=n * MIB, transcendentals=0),
    )(*args)


def run_prepare(*weights):
    weights = [pltpu.with_memory_space_constraint(w, pltpu.HBM) for w in weights]
    return pl.pallas_call(
        prepare_kernel,
        out_shape=[
            jax.ShapeDtypeStruct((1, 128), F32),
            jax.ShapeDtypeStruct((1, 128), F32),
            jax.ShapeDtypeStruct((128, 256), BF16),
            jax.ShapeDtypeStruct((256, 256), BF16),
            jax.ShapeDtypeStruct((1, 256), F32),
        ],
        in_specs=[HBM] * 4,
        out_specs=[VMEM] * 5,
        scratch_shapes=[
            pltpu.VMEM((128,), F32),
            pltpu.VMEM((128,), F32),
            pltpu.VMEM((128, 128), BF16),
            pltpu.SemaphoreType.DMA((4,)),
        ],
        compiler_params=pltpu.CompilerParams(vmem_limit_bytes=4 * MIB),
    )(*weights)


def run_right(here, pieces, gain, bias, weight):
    return pl.pallas_call(
        right_kernel,
        out_shape=jax.ShapeDtypeStruct((16, 8192), BF16),
        in_specs=[SMEM] + [VMEM] * 7,
        out_specs=VMEM,
        scratch_shapes=[pltpu.VMEM((16, 64, 128), BF16), pltpu.VMEM((64, 16, 128), F32)],
        compiler_params=pltpu.CompilerParams(vmem_limit_bytes=8 * MIB),
    )(here, *pieces, gain, bias, weight)


def run_left(here, left_0, left_1, gain, bias, weight, w_out, out_gain, out_bias):
    spread = np.zeros((256, 64), np.float32)
    spread[np.arange(256), np.arange(256) // 4] = 1
    order = np.zeros((32, 2, 4, 128), np.float32)
    for n, h in enumerate(hidden_order()):
        order[n // 4, :, n % 4, h] = 1
    return pl.pallas_call(
        left_kernel,
        out_shape=[
            jax.ShapeDtypeStruct((32, 256, 256), BF16),
            jax.ShapeDtypeStruct((256, 256), BF16),
            jax.ShapeDtypeStruct((32, 8, 128), F32),
            jax.ShapeDtypeStruct((32, 8, 128), F32),
        ],
        in_specs=[SMEM] + [VMEM] * 11,
        out_specs=[VMEM] * 4,
        scratch_shapes=[
            pltpu.VMEM((4, 16, 64, 128), BF16),
            pltpu.VMEM((4, 64, 16, 128), F32),
            pltpu.VMEM((64, 8192), BF16),
        ],
        compiler_params=pltpu.CompilerParams(vmem_limit_bytes=20 * MIB),
        cost_estimate=pl.CostEstimate(flops=4 * 10**9, bytes_accessed=12 * MIB, transcendentals=0),
    )(
        here, left_0, left_1, jnp.full((128, 128), 1 / 128, BF16), gain, bias, weight, jnp.asarray(spread, BF16), jnp.asarray(order.reshape(256, 128)),
        w_out, out_gain.reshape(1, 128), out_bias.reshape(1, 128),
    )


def run_gate(first, rows, pair, wide, shift):
    average = jnp.kron(jnp.eye(2, dtype=BF16), jnp.full((128, 128), 1 / 128, BF16))
    return pl.pallas_call(
        functools.partial(gate_kernel, first // 16),
        out_shape=pltpu.HBM((rows, 512, 128), BF16),
        in_specs=[HBM, VMEM, VMEM, VMEM],
        out_specs=HBM,
        compiler_params=pltpu.CompilerParams(vmem_limit_bytes=24 * MIB),
        cost_estimate=pl.CostEstimate(flops=rows * 2 * 10**8, bytes_accessed=MIB, transcendentals=0),
    )(pltpu.with_memory_space_constraint(pair, pltpu.HBM), average, wide, shift)


def place(near, far, x, own, first, other):
    if x == 0:
        if near == 0 or far == 0:
            return own(near, far), 0
        if far != 2:
            return f"{first}{far}", (near - 1) * 16
        return (f"P{first}1", 16 + near * 16) if near < 3 else (f"P{first}3", 32)
    if far == 0:
        if near == 0:
            return "X0", 0
        return (f"{other}3", 64) if near == 3 else ("X2", (near - 1) * 16)
    if far != 2:
        if near == 0:
            return f"{first}{far}", 48
        if near == 2:
            return "X3", 0 if far == 1 else 16
        return f"P{first}{far}", 0 if near == 1 else 16
    if near == 0:
        return f"P{first}3", 48
    return (f"Q{first}1", (near - 1) * 16) if near < 3 else (f"Q{first}3", 0)


def place_a(z, y, x):
    own = lambda near, far: f"Z{far}" if near == 0 and far else f"Y{near}"
    name, row = place(y, z, x, own, "A", "B")
    return name, row, 0


def place_b(z, y, x):
    own = lambda near, far: f"Y{far}" if near == 0 and far else (f"Z{near}" if near else "Y0")
    name, row = place(z, y, x, own, "B", "A")
    return name, row, 4096 if name[0] in "XYZ" else 0


EARLY = [(z, y, 0) for z in (0, 1, 3) for y in (0, 1, 3)] + [(2, 0, 0), (0, 2, 0)]
EARLY += [(0, 0, 1), (1, 0, 1), (3, 0, 1), (0, 1, 1), (0, 3, 1)]
LATE = [(2, 1, 1), (2, 2, 1), (2, 3, 1), (1, 2, 1), (3, 2, 1)]
OTHERS = [
    (z, y, x)
    for x in range(2)
    for z in range(4)
    for y in range(4)
    if (z, y, x) not in LATE and (z, y, x) not in EARLY
]


def per_device(
    pair_block, left_panel, right_panel, ln_gain, ln_bias, w_left, w_right, w_gate, out_gain, out_bias, w_out
):
    row = lax.axis_index("row")
    z, y, x = row // 8, (row // 2) % 4, row % 2
    c = lax.axis_index("col")

    here = jnp.stack([z, y, x, c]).astype(jnp.int32)

    parts = [lax.dynamic_slice_in_dim(right_panel, ((c + s) % 4) * 16, 16, 0) for s in range(4)]
    parts, weights = lax.optimization_barrier((parts, (ln_gain, ln_bias, w_right, w_gate)))
    gain, bias, weight, wide, shift = run_prepare(*weights)
    pieces = []
    for s in range(4):
        pairs = [(device_id(z_, y_, x_, c_), device_id(c_ + s, y_, x_, z_)) for z_, y_, x_, c_ in DEVICES]
        pieces.append(lax.ppermute(parts[s], AXES, pairs))
    rows = run_right(here, pieces, gain, bias, weight)
    rows, wide, shift = lax.optimization_barrier((rows, wide, shift))
    wide_gate = (wide, shift)

    def cat(*parts):
        return jnp.concatenate(parts, 0)

    got = {}
    def together(*names, more=()):
        held = lax.optimization_barrier([got[n] for n in names] + list(more))
        got.update(zip(names, held))
        return held[len(names) :]

    def call(blocks, before):
        names = sorted({p(*d)[0] for d in blocks for p in (place_a, place_b)})
        found = []
        for d in blocks:
            places = [p(*d) for p in (place_a, place_b)]
            found.append((d, [(names.index(name), row, lane) for name, row, lane in places]))
        sources = [got[n] for n in names]
        return run_update(found, here, sources, gates, lbd, wide_out, gain_out, bias_out, before)

    def halves(a, b):
        return jnp.concatenate([a, b], 1)

    got["Y0"] = rows
    got["X0"] = move(rows, dx=1)
    for step in (1, 3):
        got[f"Y{step}"], got[f"Z{step}"] = move(rows, dy=-step), move(rows, dz=-step)
    got["X0"], again = lax.optimization_barrier((got["X0"], rows))
    got["Y2"] = move(again, dy=2)
    got["Y1"], again = lax.optimization_barrier((got["Y1"], again))
    got["Z2"] = move(again, dz=2)
    got["Y3"], again = lax.optimization_barrier((got["Y3"], left_panel))
    left_2 = move(again, dc=2)
    gate_0 = run_gate(0, GATE_FIRST, pair_block, *wide_gate)
    ones = ("Y1", "Y2", "Y3", "Z1", "Z2", "Z3", "X0")
    (gate_0,) = together(*ones, more=[gate_0])
    half_a = [got[n][:, :4096] for n in ones]
    half_b = [got[n][:, 4096:] for n in ones]
    to_z, to_y = cat(*half_a[:3], half_a[6]), cat(*half_b[3:])
    got["A1"], got["A3"] = move(to_z, dz=-1), move(cat(to_z, half_b[6]), dz=1)
    got["B1"], got["B3"] = move(to_y, dy=-1), move(cat(to_y, half_a[6]), dy=1)
    got["X2"] = move(halves(cat(*half_a[:2]), cat(*half_b[3:5])), dx=1)
    left_0 = jnp.stack([left_panel, left_2])
    left_1 = move(left_0, dc=1)
    gate_1 = run_gate(GATE_FIRST, 64 - GATE_FIRST, pair_block, *wide_gate)
    lbd, wide_out, gain_out, bias_out = run_left(
        here, left_0, left_1, gain, bias, w_left, w_out, out_gain, out_bias
    )
    gate_1, lbd = together("A1", "A3", "B1", "B3", "X2", more=[gate_1, lbd])
    gates = (gate_0, gate_1)
    a1, a3, b1, b3, x2 = (got[n] for n in ("A1", "A3", "B1", "B3", "X2"))
    xa, xb = cat(x2[:16, :4096], b3[64:]), cat(x2[:16, 4096:], a3[64:])
    got["PA1"], got["PA3"] = move(cat(xa, a1[:32]), dz=-1), move(cat(xa, a3[32:64]), dz=1)
    got["PB1"], got["PB3"] = move(cat(xb, b1[:32]), dy=-1), move(cat(xb, b3[32:64]), dy=1)
    got["X3"] = move(halves(cat(a1[16:32], a3[16:32]), cat(b1[16:32], b3[16:32])), dx=1)
    out = call(EARLY, None)
    (out,) = together("PA1", "PA3", "PB1", "PB3", "X3", more=[out])
    x3 = got["X3"]
    got["QA1"], got["QA3"] = move(cat(got["PA1"][:16], x3[:16, :4096]), dz=-1), move(got["PA3"][16:32], dz=1)
    got["QB1"], got["QB3"] = move(cat(got["PB1"][:16], x3[:16, 4096:]), dy=-1), move(got["PB3"][16:32], dy=1)
    out = call(OTHERS[:8], out)
    (out,) = together("QA1", "QA3", "QB1", "QB3", more=[out])
    return call(LATE + OTHERS[8:], out)


def solution(mesh):
    part = P("row", "col", None)
    in_specs = (part, part, part) + (P(),) * 8
    return jax.shard_map(per_device, mesh=mesh, in_specs=in_specs, out_specs=part, check_vma=False)
```

```python
import functools

import jax
import jax.numpy as jnp
import numpy as np
from jax import lax
from jax.experimental import pallas as pl
from jax.experimental.pallas import tpu as pltpu
from jax.sharding import PartitionSpec as P

AXES = ("row", "col")
BF16, F32 = jnp.bfloat16, jnp.float32
DEVICES = [(z, y, x, c) for z in range(4) for y in range(4) for x in range(2) for c in range(4)]
MIB = 1 << 20
PARTS = 4
GATE_FIRST = 16


def device_id(z, y, x, c):
    return (((z % 4) * 4 + y % 4) * 2 + x % 2) * 4 + c


def move(value, dz=0, dy=0, dx=0, dc=0):
    pairs = [
        (device_id(z, y, x, c), device_id(z + dz, y + dy, x + dx, c ^ dc)) for z, y, x, c in DEVICES
    ]
    return lax.ppermute(value, AXES, pairs)


def sigmoid(values):
    return 0.5 * jnp.tanh(0.5 * values) + 0.5


def hidden_order():
    order = []
    for group in range(32):
        first = 2 * group
        order += [first, first + 64, first + 1, first + 65]
    return np.array(order)


def standardize(values, average):
    mean = jnp.dot(values, average, preferred_element_type=F32)
    centered = values.astype(F32) - mean
    var = jnp.dot((centered * centered).astype(BF16), average, preferred_element_type=F32)
    return centered * lax.rsqrt(var + 1e-05)


def scale(values, gain, bias):
    return (values * gain.reshape(1, 128) + bias.reshape(1, 128)).astype(BF16)


def project_16(normed, weight, swap, store):
    proj = lax.dot_general(
        weight, normed.reshape(16 * 64, 128), (((0,), (1,)), ((), ())), preferred_element_type=F32
    )
    value = (sigmoid(proj[:128]) * proj[128:]).astype(BF16).astype(F32)
    low, high = value[:64], value[64:]
    lane = lax.broadcasted_iota(jnp.int32, (64, 128), 1)
    for pair in range(8):
        lo = low[:, pair * 128 : (pair + 1) * 128]
        hi = high[:, pair * 128 : (pair + 1) * 128]
        swap[:, 2 * pair, :] = jnp.where(lane < 64, lo, pltpu.roll(hi, 64, 1))
        swap[:, 2 * pair + 1, :] = jnp.where(lane < 64, pltpu.roll(lo, 64, 1), hi)
    for h in range(64):
        store(h, swap[h].astype(BF16))


def prepare_kernel(gain_in, bias_in, right_in, gate_in, gain, bias, right, wide, shift, gain_row, bias_row, gate, sem):
    pairs = ((gain_in, gain_row), (bias_in, bias_row), (right_in, right), (gate_in, gate))
    fetches = [pltpu.make_async_copy(source, target, sem.at[n]) for n, (source, target) in enumerate(pairs)]
    for fetch in fetches:
        fetch.start()
    for fetch in fetches:
        fetch.wait()
    gain[...] = gain_row[...].reshape(1, 128)
    bias[...] = bias_row[...].reshape(1, 128)
    half = 0.5 * gate[...].astype(F32)
    block = (jnp.broadcast_to(gain[...], (128, 128)).T * half).astype(BF16)
    wide[...] = jnp.zeros((256, 256), BF16)
    wide[:128, :128] = block
    wide[128:, 128:] = block
    rows = jnp.broadcast_to(bias[...], (8, 128))
    made = jnp.dot(rows, half, preferred_element_type=F32, precision=lax.Precision.HIGHEST)[:1]
    shift[:, :128] = made
    shift[:, 128:] = made


def right_kernel(here, p0, p1, p2, p3, gain, bias, weight, out, normed, swap):
    average = jnp.full((128, 128), 1 / 128, BF16)
    for s, piece in enumerate((p0, p1, p2, p3)):
        start = pl.multiple_of(lax.rem(here[0] - s + 4, 4) * 16, 16)
        made = scale(standardize(piece[...].reshape(256, 128), average), gain[...], bias[...])
        normed[:, pl.ds(start, 16), :] = made.reshape(16, 16, 128)

    def store(h, tile):
        out[:, h * 128 : (h + 1) * 128] = tile

    project_16(normed[...], weight[...], swap, store)


def left_kernel(
    here, left_0, left_1, average, gain, bias, weight, spread, order, w_out, out_gain, out_bias,
    out, wide_out, shift, normed, swap, rows,
):
    for quarter in range(4):
        at = slice(quarter * 16, quarter * 16 + 16)
        mine = normed.at[quarter]
        for flip in range(4):
            piece = (left_0, left_1)[flip % 2][flip // 2, at].reshape(256, 128)
            start = pl.multiple_of((here[3] ^ flip) * 16, 16)
            made = scale(standardize(piece, average[...]), gain[...], bias[...])
            mine[:, pl.ds(start, 16), :] = made.reshape(16, 16, 128)

        def store(h, tile, at=at):
            rows[at, h * 128 : (h + 1) * 128] = tile

        project_16(mine[...], weight[...], swap.at[quarter], store)
    row = lax.broadcasted_iota(jnp.int32, (256, 256), 0)
    lane = lax.broadcasted_iota(jnp.int32, (256, 256), 1)
    keep = lax.rem(row, 4) == lane // 64

    def body(g, carry):
        tile = rows[:, pl.ds(pl.multiple_of(g * 256, 256), 256)]
        wide = jnp.dot(spread[...], tile, preferred_element_type=F32)
        out[g] = jnp.where(keep, wide, 0.0).astype(BF16)
        return carry

    lax.fori_loop(0, 32, body, 0, unroll=32)
    weight_out = w_out[...].astype(F32)
    scaled = jnp.broadcast_to(out_gain[...], (128, 128)).T * weight_out
    made = jnp.dot(order[...], scaled.astype(BF16), preferred_element_type=F32)
    second = lax.rem(lax.broadcasted_iota(jnp.int32, (256, 128), 0), 8) // 4
    wide_out[:, :128] = jnp.where(second == 0, made, 0.0).astype(BF16)
    wide_out[:, 128:] = jnp.where(second == 1, made, 0.0).astype(BF16)
    rows_bias = jnp.broadcast_to(out_bias[...], (8, 128))
    made = jnp.dot(rows_bias, weight_out, preferred_element_type=F32, precision=lax.Precision.HIGHEST)[:1]
    shift[:, :128] = made
    shift[:, 128:] = made


def gate_block(average, weight, bias, pair, out):
    for i in range(0, pair.shape[0], 2):
        both = jnp.concatenate([pair[i], pair[i + 1]], 1)
        mean = jnp.dot(both, average[...], preferred_element_type=F32)
        centered = (both.astype(F32) - mean).astype(BF16)
        var = jnp.dot(centered * centered, average[...], preferred_element_type=F32)
        proj = jnp.dot(centered, weight[...], preferred_element_type=F32)
        proj = proj * lax.rsqrt(var + 1e-05) + bias[...]
        gate = (0.5 * jnp.tanh(proj) + 0.5).astype(BF16)
        out[i], out[i + 1] = gate[:, :128], gate[:, 128:]


def gate_kernel(first, pair, average, weight, bias, out):
    pltpu.emit_pipeline(
        functools.partial(gate_block, average, weight, bias),
        grid=(out.shape[0] // 16,),
        in_specs=[pl.BlockSpec((16, 512, 128), lambda n: (n + first, 0, 0))],
        out_specs=[pl.BlockSpec((16, 512, 128), lambda n: (n, 0, 0))],
    )(pair, out)


def update_kernel(blocks, n_src, has_out, *refs):
    here = refs[0]
    sources = refs[1 : 1 + n_src]
    gate_0, gate_1, lbd, wide_out, shift = refs[1 + n_src : 6 + n_src]
    refs = refs[6 + n_src + has_out :]
    out, product, gates, results, gate_sem, out_sem = refs
    z, y, x = here[0], here[1], here[2]
    columns = 16 * len(blocks)

    def column(b):
        dz, dy, dx = blocks[b][0]
        start = (lax.rem(y + dy, 4) * 2 + lax.rem(x + dx, 2)) * 64 + lax.rem(z + dz, 4) * 16
        return pl.ds(pl.multiple_of(start, 16), 16)

    def gate_copy(b, half):
        return pltpu.make_async_copy(
            (gate_0, gate_1)[half].at[:, column(b), :],
            gates.at[pl.ds(half * GATE_FIRST, (GATE_FIRST, 64 - GATE_FIRST)[half]), pl.ds(b * 16, 16), :],
            gate_sem.at[b, half],
        )

    def out_copy(b, q):
        rows = pl.ds(q * 64 // PARTS, 64 // PARTS)
        return pltpu.make_async_copy(
            results.at[rows, pl.ds(b * 16, 16), :], out.at[rows, column(b), :], out_sem.at[b, q]
        )

    for b in range(len(blocks)):
        gate_copy(b, 0).start()
        gate_copy(b, 1).start()
    member = lax.broadcasted_iota(jnp.int32, (8, 128), 0)

    def over_four(total):
        swapped = jnp.where(lax.rem(member, 2) == 0, pltpu.roll(total, 7, 0), pltpu.roll(total, 1, 0))
        total = total + swapped
        swapped = jnp.where(lax.rem(member, 4) < 2, pltpu.roll(total, 6, 0), pltpu.roll(total, 2, 0))
        return total + swapped

    for half in range(2):

        def multiply(g, carry, half=half):
            parts = []
            for _, halves in blocks:
                src, row, lane = halves[half]
                at = pl.ds(pl.multiple_of(lane + g * 256, 256), 256)
                parts.append(sources[src][row : row + 16, at])
            made = lax.dot_general(
                lbd[half * 16 + g],
                jnp.concatenate(parts, 0),
                (((1,), (1,)), ((), ())),
                preferred_element_type=F32,
            )
            product[:, half * 16 + g] = made.reshape(32, 8, columns)
            return carry

        lax.fori_loop(0, 16, multiply, 0, unroll=16)
    for b in range(len(blocks)):
        gate_copy(b, 0).wait()
        gate_copy(b, 1).wait()

    def finish(ip, carry):
        for part in range(columns // 128):
            lanes = slice(part * 128, part * 128 + 128)
            values = product[ip, :, :, lanes]
            mean = over_four(jnp.sum(values, axis=0)) * (1.0 / 128)
            centered = values - mean[None]
            var = over_four(jnp.sum(centered * centered, axis=0)) * (1.0 / 128)
            normed = centered * lax.rsqrt(var + 1e-05)[None]
            normed = normed.reshape(256, 128).astype(BF16)
            both = lax.dot_general(
                normed, wide_out[...], (((0,), (0,)), ((), ())), preferred_element_type=F32
            )
            both = both + shift[...]
            for i2 in range(2):
                row = 2 * ip + i2
                gate = gates[row, lanes].astype(F32)
                results[row, lanes] = (both[:, i2 * 128 : (i2 + 1) * 128] * gate).astype(BF16)
        return carry

    for q in range(PARTS):
        lax.fori_loop(q * 32 // PARTS, (q + 1) * 32 // PARTS, finish, 0, unroll=8)
        for b in range(len(blocks)):
            out_copy(b, q).start()
    for b in range(len(blocks)):
        for q in range(PARTS):
            out_copy(b, q).wait()


VMEM = pl.BlockSpec(memory_space=pltpu.VMEM)
SMEM = pl.BlockSpec(memory_space=pltpu.SMEM)
HBM = pl.BlockSpec(memory_space=pltpu.HBM)


def run_update(blocks, here, sources, gates, lbd, wide_out, shift, before):
    n = len(blocks)
    has_out = before is not None
    args = [here, *sources, *gates, lbd, wide_out, shift] + ([before] if has_out else [])
    return pl.pallas_call(
        functools.partial(update_kernel, blocks, len(sources), has_out),
        out_shape=pltpu.HBM((64, 512, 128), BF16),
        in_specs=[SMEM] + [VMEM] * len(sources) + [HBM] * 2 + [VMEM] * 3 + [HBM] * has_out,
        out_specs=HBM,
        scratch_shapes=[
            pltpu.VMEM((32, 32, 8, n * 16), F32),
            pltpu.VMEM((64, n * 16, 128), BF16),
            pltpu.VMEM((64, n * 16, 128), BF16),
            pltpu.SemaphoreType.DMA((n, 2)),
            pltpu.SemaphoreType.DMA((n, PARTS)),
        ],
        input_output_aliases={len(args) - 1: 0} if has_out else {},
        compiler_params=pltpu.CompilerParams(vmem_limit_bytes=(8 + 5 * n // 4) * MIB),
        cost_estimate=pl.CostEstimate(flops=n * 4 * 10**8, bytes_accessed=n * MIB, transcendentals=0),
    )(*args)


def run_prepare(*weights):
    weights = [pltpu.with_memory_space_constraint(w, pltpu.HBM) for w in weights]
    return pl.pallas_call(
        prepare_kernel,
        out_shape=[
            jax.ShapeDtypeStruct((1, 128), F32),
            jax.ShapeDtypeStruct((1, 128), F32),
            jax.ShapeDtypeStruct((128, 256), BF16),
            jax.ShapeDtypeStruct((256, 256), BF16),
            jax.ShapeDtypeStruct((1, 256), F32),
        ],
        in_specs=[HBM] * 4,
        out_specs=[VMEM] * 5,
        scratch_shapes=[
            pltpu.VMEM((128,), F32),
            pltpu.VMEM((128,), F32),
            pltpu.VMEM((128, 128), BF16),
            pltpu.SemaphoreType.DMA((4,)),
        ],
        compiler_params=pltpu.CompilerParams(vmem_limit_bytes=4 * MIB),
    )(*weights)


def run_right(here, pieces, gain, bias, weight):
    return pl.pallas_call(
        right_kernel,
        out_shape=jax.ShapeDtypeStruct((16, 8192), BF16),
        in_specs=[SMEM] + [VMEM] * 7,
        out_specs=VMEM,
        scratch_shapes=[pltpu.VMEM((16, 64, 128), BF16), pltpu.VMEM((64, 16, 128), F32)],
        compiler_params=pltpu.CompilerParams(vmem_limit_bytes=8 * MIB),
    )(here, *pieces, gain, bias, weight)


def run_left(here, left_0, left_1, gain, bias, weight, w_out, out_gain, out_bias):
    spread = np.zeros((256, 64), np.float32)
    spread[np.arange(256), np.arange(256) // 4] = 1
    order = np.zeros((32, 2, 4, 128), np.float32)
    for n, h in enumerate(hidden_order()):
        order[n // 4, :, n % 4, h] = 1
    return pl.pallas_call(
        left_kernel,
        out_shape=[
            jax.ShapeDtypeStruct((32, 256, 256), BF16),
            jax.ShapeDtypeStruct((256, 256), BF16),
            jax.ShapeDtypeStruct((1, 256), F32),
        ],
        in_specs=[SMEM] + [VMEM] * 11,
        out_specs=[VMEM] * 3,
        scratch_shapes=[
            pltpu.VMEM((4, 16, 64, 128), BF16),
            pltpu.VMEM((4, 64, 16, 128), F32),
            pltpu.VMEM((64, 8192), BF16),
        ],
        compiler_params=pltpu.CompilerParams(vmem_limit_bytes=20 * MIB),
        cost_estimate=pl.CostEstimate(flops=4 * 10**9, bytes_accessed=12 * MIB, transcendentals=0),
    )(
        here, left_0, left_1, jnp.full((128, 128), 1 / 128, BF16), gain, bias, weight, jnp.asarray(spread, BF16), jnp.asarray(order.reshape(256, 128), BF16),
        w_out, out_gain.reshape(1, 128), out_bias.reshape(1, 128),
    )


def run_gate(first, rows, pair, wide, shift):
    average = jnp.kron(jnp.eye(2, dtype=BF16), jnp.full((128, 128), 1 / 128, BF16))
    return pl.pallas_call(
        functools.partial(gate_kernel, first // 16),
        out_shape=pltpu.HBM((rows, 512, 128), BF16),
        in_specs=[HBM, VMEM, VMEM, VMEM],
        out_specs=HBM,
        compiler_params=pltpu.CompilerParams(vmem_limit_bytes=24 * MIB),
        cost_estimate=pl.CostEstimate(flops=rows * 2 * 10**8, bytes_accessed=MIB, transcendentals=0),
    )(pltpu.with_memory_space_constraint(pair, pltpu.HBM), average, wide, shift)


def place(near, far, x, own, first, other):
    if x == 0:
        if near == 0 or far == 0:
            return own(near, far), 0
        if far != 2:
            return f"{first}{far}", (near - 1) * 16
        return (f"P{first}1", 16 + near * 16) if near < 3 else (f"P{first}3", 32)
    if far == 0:
        if near == 0:
            return "X0", 0
        return (f"{other}3", 64) if near == 3 else ("X2", (near - 1) * 16)
    if far != 2:
        if near == 0:
            return f"{first}{far}", 48
        if near == 2:
            return "X3", 0 if far == 1 else 16
        return f"P{first}{far}", 0 if near == 1 else 16
    if near == 0:
        return f"P{first}3", 48
    return (f"Q{first}1", (near - 1) * 16) if near < 3 else ("X4", 0)


def place_a(z, y, x):
    own = lambda near, far: f"Z{far}" if near == 0 and far else f"Y{near}"
    name, row = place(y, z, x, own, "A", "B")
    return name, row, 0


def place_b(z, y, x):
    own = lambda near, far: f"Y{far}" if near == 0 and far else (f"Z{near}" if near else "Y0")
    name, row = place(z, y, x, own, "B", "A")
    return name, row, 4096 if name[0] in "XYZ" else 0


EARLY = [(z, y, 0) for z in (0, 1, 3) for y in (0, 1, 3)] + [(2, 0, 0), (0, 2, 0)]
EARLY += [(0, 0, 1), (1, 0, 1), (3, 0, 1), (0, 1, 1), (0, 3, 1)]
LATE = [(2, 1, 1), (2, 2, 1), (2, 3, 1), (1, 2, 1), (3, 2, 1)]
OTHERS = [
    (z, y, x)
    for x in range(2)
    for z in range(4)
    for y in range(4)
    if (z, y, x) not in LATE and (z, y, x) not in EARLY
]


def per_device(
    pair_block, left_panel, right_panel, ln_gain, ln_bias, w_left, w_right, w_gate, out_gain, out_bias, w_out
):
    row = lax.axis_index("row")
    z, y, x = row // 8, (row // 2) % 4, row % 2
    c = lax.axis_index("col")

    here = jnp.stack([z, y, x, c]).astype(jnp.int32)

    parts = [lax.dynamic_slice_in_dim(right_panel, ((c + s) % 4) * 16, 16, 0) for s in range(4)]
    parts, weights = lax.optimization_barrier((parts, (ln_gain, ln_bias, w_right, w_gate)))
    gain, bias, weight, wide, shift = run_prepare(*weights)
    pieces = []
    for s in range(4):
        pairs = [(device_id(z_, y_, x_, c_), device_id(c_ + s, y_, x_, z_)) for z_, y_, x_, c_ in DEVICES]
        pieces.append(lax.ppermute(parts[s], AXES, pairs))
    rows = run_right(here, pieces, gain, bias, weight)
    rows, wide, shift = lax.optimization_barrier((rows, wide, shift))
    wide_gate = (wide, shift)

    def cat(*parts):
        return jnp.concatenate(parts, 0)

    got = {}
    def together(*names, more=()):
        held = lax.optimization_barrier([got[n] for n in names] + list(more))
        got.update(zip(names, held))
        return held[len(names) :]

    def call(blocks, before):
        names = sorted({p(*d)[0] for d in blocks for p in (place_a, place_b)})
        found = []
        for d in blocks:
            places = [p(*d) for p in (place_a, place_b)]
            found.append((d, [(names.index(name), row, lane) for name, row, lane in places]))
        sources = [got[n] for n in names]
        return run_update(found, here, sources, gates, lbd, wide_out, shift_out, before)

    def halves(a, b):
        return jnp.concatenate([a, b], 1)

    got["Y0"] = rows
    got["X0"] = move(rows, dx=1)
    for step in (1, 3):
        got[f"Y{step}"], got[f"Z{step}"] = move(rows, dy=-step), move(rows, dz=-step)
    got["X0"], again = lax.optimization_barrier((got["X0"], rows))
    got["Y2"] = move(again, dy=2)
    got["Y1"], again = lax.optimization_barrier((got["Y1"], again))
    got["Z2"] = move(again, dz=2)
    got["Y3"], again = lax.optimization_barrier((got["Y3"], left_panel))
    left_2 = move(again, dc=2)
    gate_0 = run_gate(0, GATE_FIRST, pair_block, *wide_gate)
    ones = ("Y1", "Y2", "Y3", "Z1", "Z2", "Z3", "X0")
    (gate_0,) = together(*ones, more=[gate_0])
    half_a = [got[n][:, :4096] for n in ones]
    half_b = [got[n][:, 4096:] for n in ones]
    to_z, to_y = cat(*half_a[:3], half_a[6]), cat(*half_b[3:])
    got["A1"], got["A3"] = move(to_z, dz=-1), move(cat(to_z, half_b[6]), dz=1)
    got["B1"], got["B3"] = move(to_y, dy=-1), move(cat(to_y, half_a[6]), dy=1)
    got["X2"] = move(halves(cat(*half_a[:2]), cat(*half_b[3:5])), dx=1)
    left_0 = jnp.stack([left_panel, left_2])
    left_1 = move(left_0, dc=1)
    gate_1 = run_gate(GATE_FIRST, 64 - GATE_FIRST, pair_block, *wide_gate)
    lbd, wide_out, shift_out = run_left(
        here, left_0, left_1, gain, bias, w_left, w_out, out_gain, out_bias
    )
    gate_1, lbd = together("A1", "A3", "B1", "B3", "X2", more=[gate_1, lbd])
    gates = (gate_0, gate_1)
    a1, a3, b1, b3, x2 = (got[n] for n in ("A1", "A3", "B1", "B3", "X2"))
    xa, xb = cat(x2[:16, :4096], b3[64:]), cat(x2[:16, 4096:], a3[64:])
    got["PA1"], got["PA3"] = move(cat(xa, a1[:32]), dz=-1), move(cat(xa, a3[32:64]), dz=1)
    got["PB1"], got["PB3"] = move(cat(xb, b1[:32]), dy=-1), move(cat(xb, b3[32:64]), dy=1)
    got["X3"] = move(halves(cat(a1[16:32], a3[16:32]), cat(b1[16:32], b3[16:32])), dx=1)
    out = call(EARLY, None)
    (out,) = together("PA1", "PA3", "PB1", "PB3", "X3", more=[out])
    x3 = got["X3"]
    got["QA1"] = move(cat(got["PA1"][:16], x3[:16, :4096]), dz=-1)
    got["QB1"] = move(cat(got["PB1"][:16], x3[:16, 4096:]), dy=-1)
    got["X4"] = move(halves(got["PA3"][32:48], got["PB3"][32:48]), dx=1)
    out = call(OTHERS[:8], out)
    (out,) = together("QA1", "QB1", "X4", more=[out])
    return call(LATE + OTHERS[8:], out)


def solution(mesh):
    part = P("row", "col", None)
    in_specs = (part, part, part) + (P(),) * 8
    return jax.shard_map(per_device, mesh=mesh, in_specs=in_specs, out_specs=part, check_vma=False)
```

```python
import functools

import jax
import jax.numpy as jnp
import numpy as np
from jax import lax
from jax.experimental import pallas as pl
from jax.experimental.pallas import tpu as pltpu
from jax.sharding import PartitionSpec as P

AXES = ("row", "col")
BF16, F32 = jnp.bfloat16, jnp.float32
DEVICES = [(z, y, x, c) for z in range(4) for y in range(4) for x in range(2) for c in range(4)]
MIB = 1 << 20
PARTS = 4
GATE_FIRST = 16


def device_id(z, y, x, c):
    return (((z % 4) * 4 + y % 4) * 2 + x % 2) * 4 + c


def move(value, dz=0, dy=0, dx=0, dc=0):
    pairs = [
        (device_id(z, y, x, c), device_id(z + dz, y + dy, x + dx, c ^ dc)) for z, y, x, c in DEVICES
    ]
    return lax.ppermute(value, AXES, pairs)


def sigmoid(values):
    return 0.5 * jnp.tanh(0.5 * values) + 0.5


def hidden_order():
    order = []
    for group in range(32):
        first = 2 * group
        order += [first, first + 64, first + 1, first + 65]
    return np.array(order)


def standardize(values, average):
    mean = jnp.dot(values, average, preferred_element_type=F32)
    centered = values.astype(F32) - mean
    var = jnp.dot((centered * centered).astype(BF16), average, preferred_element_type=F32)
    return centered * lax.rsqrt(var + 1e-05)


def scale(values, gain, bias):
    return (values * gain.reshape(1, 128) + bias.reshape(1, 128)).astype(BF16)


def project_16(normed, weight, swap, store):
    proj = lax.dot_general(
        weight, normed.reshape(16 * 64, 128), (((0,), (1,)), ((), ())), preferred_element_type=F32
    )
    value = (sigmoid(proj[:128]) * proj[128:]).astype(BF16).astype(F32)
    low, high = value[:64], value[64:]
    lane = lax.broadcasted_iota(jnp.int32, (64, 128), 1)
    for pair in range(8):
        lo = low[:, pair * 128 : (pair + 1) * 128]
        hi = high[:, pair * 128 : (pair + 1) * 128]
        swap[:, 2 * pair, :] = jnp.where(lane < 64, lo, pltpu.roll(hi, 64, 1))
        swap[:, 2 * pair + 1, :] = jnp.where(lane < 64, pltpu.roll(lo, 64, 1), hi)
    for h in range(64):
        store(h, swap[h].astype(BF16))


def prepare_kernel(gain_in, bias_in, right_in, gate_in, gain, bias, right, wide, shift, gain_row, bias_row, gate, sem):
    pairs = ((gain_in, gain_row), (bias_in, bias_row), (right_in, right), (gate_in, gate))
    fetches = [pltpu.make_async_copy(source, target, sem.at[n]) for n, (source, target) in enumerate(pairs)]
    for fetch in fetches:
        fetch.start()
    for fetch in fetches:
        fetch.wait()
    gain[...] = gain_row[...].reshape(1, 128)
    bias[...] = bias_row[...].reshape(1, 128)
    half = 0.5 * gate[...].astype(F32)
    block = (jnp.broadcast_to(gain[...], (128, 128)).T * half).astype(BF16)
    wide[...] = jnp.zeros((256, 256), BF16)
    wide[:128, :128] = block
    wide[128:, 128:] = block
    rows = jnp.broadcast_to(bias[...], (8, 128))
    made = jnp.dot(rows, half, preferred_element_type=F32, precision=lax.Precision.HIGHEST)[:1]
    shift[:, :128] = made
    shift[:, 128:] = made


def right_kernel(here, p0, p1, p2, p3, gain, bias, weight, out, normed, swap):
    average = jnp.full((128, 128), 1 / 128, BF16)
    for s, piece in enumerate((p0, p1, p2, p3)):
        start = pl.multiple_of(lax.rem(here[0] - s + 4, 4) * 16, 16)
        made = scale(standardize(piece[...].reshape(256, 128), average), gain[...], bias[...])
        normed[:, pl.ds(start, 16), :] = made.reshape(16, 16, 128)

    def store(h, tile):
        out[:, h * 128 : (h + 1) * 128] = tile

    project_16(normed[...], weight[...], swap, store)


def left_kernel(
    here, left_0, left_1, average, gain, bias, weight, spread, order, w_out, out_gain, out_bias,
    out, wide_out, shift, normed, swap, rows,
):
    for quarter in range(4):
        at = slice(quarter * 16, quarter * 16 + 16)
        mine = normed.at[quarter]
        for flip in range(4):
            piece = (left_0, left_1)[flip % 2][flip // 2, at].reshape(256, 128)
            start = pl.multiple_of((here[3] ^ flip) * 16, 16)
            made = scale(standardize(piece, average[...]), gain[...], bias[...])
            mine[:, pl.ds(start, 16), :] = made.reshape(16, 16, 128)

        def store(h, tile, at=at):
            rows[at, h * 128 : (h + 1) * 128] = tile

        project_16(mine[...], weight[...], swap.at[quarter], store)
    row = lax.broadcasted_iota(jnp.int32, (256, 256), 0)
    lane = lax.broadcasted_iota(jnp.int32, (256, 256), 1)
    keep = lax.rem(row, 4) == lane // 64

    def body(g, carry):
        tile = rows[:, pl.ds(pl.multiple_of(g * 256, 256), 256)]
        wide = jnp.dot(spread[...], tile, preferred_element_type=F32)
        out[g] = jnp.where(keep, wide, 0.0).astype(BF16)
        return carry

    lax.fori_loop(0, 32, body, 0, unroll=32)
    weight_out = w_out[...].astype(F32)
    scaled = jnp.broadcast_to(out_gain[...], (128, 128)).T * weight_out
    made = jnp.dot(order[...], scaled.astype(BF16), preferred_element_type=F32)
    second = lax.rem(lax.broadcasted_iota(jnp.int32, (256, 128), 0), 8) // 4
    wide_out[:, :128] = jnp.where(second == 0, made, 0.0).astype(BF16)
    wide_out[:, 128:] = jnp.where(second == 1, made, 0.0).astype(BF16)
    rows_bias = jnp.broadcast_to(out_bias[...], (8, 128))
    made = jnp.dot(rows_bias, weight_out, preferred_element_type=F32, precision=lax.Precision.HIGHEST)[:1]
    shift[:, :128] = made
    shift[:, 128:] = made


def gate_block(average, weight, bias, pair, out):
    for i in range(0, pair.shape[0], 2):
        both = jnp.concatenate([pair[i], pair[i + 1]], 1)
        mean = jnp.dot(both, average[...], preferred_element_type=F32)
        centered = (both.astype(F32) - mean).astype(BF16)
        var = jnp.dot(centered * centered, average[...], preferred_element_type=F32)
        proj = jnp.dot(centered, weight[...], preferred_element_type=F32)
        proj = proj * lax.rsqrt(var + 1e-05) + bias[...]
        gate = (0.5 * jnp.tanh(proj) + 0.5).astype(BF16)
        out[i], out[i + 1] = gate[:, :128], gate[:, 128:]


def gate_kernel(first, pair, average, weight, bias, out):
    pltpu.emit_pipeline(
        functools.partial(gate_block, average, weight, bias),
        grid=(out.shape[0] // 16,),
        in_specs=[pl.BlockSpec((16, 512, 128), lambda n: (n + first, 0, 0))],
        out_specs=[pl.BlockSpec((16, 512, 128), lambda n: (n, 0, 0))],
    )(pair, out)


def update_kernel(blocks, n_src, has_out, *refs):
    here = refs[0]
    sources = refs[1 : 1 + n_src]
    gate_0, gate_1, lbd, wide_out, shift = refs[1 + n_src : 6 + n_src]
    refs = refs[6 + n_src + has_out :]
    out, product, gates, results, gate_sem, out_sem = refs
    z, y, x = here[0], here[1], here[2]
    columns = 16 * len(blocks)

    def column(b):
        dz, dy, dx = blocks[b][0]
        start = (lax.rem(y + dy, 4) * 2 + lax.rem(x + dx, 2)) * 64 + lax.rem(z + dz, 4) * 16
        return pl.ds(pl.multiple_of(start, 16), 16)

    def gate_copy(b, half):
        return pltpu.make_async_copy(
            (gate_0, gate_1)[half].at[:, column(b), :],
            gates.at[pl.ds(half * GATE_FIRST, (GATE_FIRST, 64 - GATE_FIRST)[half]), pl.ds(b * 16, 16), :],
            gate_sem.at[b, half],
        )

    def out_copy(b, q):
        rows = pl.ds(q * 64 // PARTS, 64 // PARTS)
        return pltpu.make_async_copy(
            results.at[rows, pl.ds(b * 16, 16), :], out.at[rows, column(b), :], out_sem.at[b, q]
        )

    for half in range(2):
        for b in range(len(blocks)):
            gate_copy(b, half).start()
    member = lax.broadcasted_iota(jnp.int32, (8, 128), 0)

    def over_four(total):
        swapped = jnp.where(lax.rem(member, 2) == 0, pltpu.roll(total, 7, 0), pltpu.roll(total, 1, 0))
        total = total + swapped
        swapped = jnp.where(lax.rem(member, 4) < 2, pltpu.roll(total, 6, 0), pltpu.roll(total, 2, 0))
        return total + swapped

    for half in range(2):

        def multiply(g, carry, half=half):
            parts = []
            for _, halves in blocks:
                src, row, lane = halves[half]
                at = pl.ds(pl.multiple_of(lane + g * 256, 256), 256)
                parts.append(sources[src][row : row + 16, at])
            made = lax.dot_general(
                lbd[half * 16 + g],
                jnp.concatenate(parts, 0),
                (((1,), (1,)), ((), ())),
                preferred_element_type=F32,
            )
            product[:, half * 16 + g] = made.reshape(32, 8, columns)
            return carry

        lax.fori_loop(0, 16, multiply, 0, unroll=16)
    def finish(ip, carry):
        for part in range(columns // 128):
            lanes = slice(part * 128, part * 128 + 128)
            values = product[ip, :, :, lanes]
            mean = over_four(jnp.sum(values, axis=0)) * (1.0 / 128)
            centered = values - mean[None]
            var = over_four(jnp.sum(centered * centered, axis=0)) * (1.0 / 128)
            normed = centered * lax.rsqrt(var + 1e-05)[None]
            normed = normed.reshape(256, 128).astype(BF16)
            both = lax.dot_general(
                normed, wide_out[...], (((0,), (0,)), ((), ())), preferred_element_type=F32
            )
            both = both + shift[...]
            for i2 in range(2):
                row = 2 * ip + i2
                gate = gates[row, lanes].astype(F32)
                results[row, lanes] = (both[:, i2 * 128 : (i2 + 1) * 128] * gate).astype(BF16)
        return carry

    for q in range(PARTS):
        if q < 2:
            for b in range(len(blocks)):
                gate_copy(b, q).wait()
        lax.fori_loop(q * 32 // PARTS, (q + 1) * 32 // PARTS, finish, 0, unroll=8)
        for b in range(len(blocks)):
            out_copy(b, q).start()
    for b in range(len(blocks)):
        for q in range(PARTS):
            out_copy(b, q).wait()


VMEM = pl.BlockSpec(memory_space=pltpu.VMEM)
SMEM = pl.BlockSpec(memory_space=pltpu.SMEM)
HBM = pl.BlockSpec(memory_space=pltpu.HBM)


def run_update(blocks, here, sources, gates, lbd, wide_out, shift, before):
    n = len(blocks)
    has_out = before is not None
    args = [here, *sources, *gates, lbd, wide_out, shift] + ([before] if has_out else [])
    return pl.pallas_call(
        functools.partial(update_kernel, blocks, len(sources), has_out),
        out_shape=pltpu.HBM((64, 512, 128), BF16),
        in_specs=[SMEM] + [VMEM] * len(sources) + [HBM] * 2 + [VMEM] * 3 + [HBM] * has_out,
        out_specs=HBM,
        scratch_shapes=[
            pltpu.VMEM((32, 32, 8, n * 16), F32),
            pltpu.VMEM((64, n * 16, 128), BF16),
            pltpu.VMEM((64, n * 16, 128), BF16),
            pltpu.SemaphoreType.DMA((n, 2)),
            pltpu.SemaphoreType.DMA((n, PARTS)),
        ],
        input_output_aliases={len(args) - 1: 0} if has_out else {},
        compiler_params=pltpu.CompilerParams(vmem_limit_bytes=(8 + 5 * n // 4) * MIB),
        cost_estimate=pl.CostEstimate(flops=n * 4 * 10**8, bytes_accessed=n * MIB, transcendentals=0),
    )(*args)


def run_prepare(*weights):
    weights = [pltpu.with_memory_space_constraint(w, pltpu.HBM) for w in weights]
    return pl.pallas_call(
        prepare_kernel,
        out_shape=[
            jax.ShapeDtypeStruct((1, 128), F32),
            jax.ShapeDtypeStruct((1, 128), F32),
            jax.ShapeDtypeStruct((128, 256), BF16),
            jax.ShapeDtypeStruct((256, 256), BF16),
            jax.ShapeDtypeStruct((1, 256), F32),
        ],
        in_specs=[HBM] * 4,
        out_specs=[VMEM] * 5,
        scratch_shapes=[
            pltpu.VMEM((128,), F32),
            pltpu.VMEM((128,), F32),
            pltpu.VMEM((128, 128), BF16),
            pltpu.SemaphoreType.DMA((4,)),
        ],
        compiler_params=pltpu.CompilerParams(vmem_limit_bytes=4 * MIB),
    )(*weights)


def run_right(here, pieces, gain, bias, weight):
    return pl.pallas_call(
        right_kernel,
        out_shape=jax.ShapeDtypeStruct((16, 8192), BF16),
        in_specs=[SMEM] + [VMEM] * 7,
        out_specs=VMEM,
        scratch_shapes=[pltpu.VMEM((16, 64, 128), BF16), pltpu.VMEM((64, 16, 128), F32)],
        compiler_params=pltpu.CompilerParams(vmem_limit_bytes=8 * MIB),
    )(here, *pieces, gain, bias, weight)


def run_left(here, left_0, left_1, gain, bias, weight, w_out, out_gain, out_bias):
    spread = np.zeros((256, 64), np.float32)
    spread[np.arange(256), np.arange(256) // 4] = 1
    order = np.zeros((32, 2, 4, 128), np.float32)
    for n, h in enumerate(hidden_order()):
        order[n // 4, :, n % 4, h] = 1
    return pl.pallas_call(
        left_kernel,
        out_shape=[
            jax.ShapeDtypeStruct((32, 256, 256), BF16),
            jax.ShapeDtypeStruct((256, 256), BF16),
            jax.ShapeDtypeStruct((1, 256), F32),
        ],
        in_specs=[SMEM] + [VMEM] * 11,
        out_specs=[VMEM] * 3,
        scratch_shapes=[
            pltpu.VMEM((4, 16, 64, 128), BF16),
            pltpu.VMEM((4, 64, 16, 128), F32),
            pltpu.VMEM((64, 8192), BF16),
        ],
        compiler_params=pltpu.CompilerParams(vmem_limit_bytes=20 * MIB),
        cost_estimate=pl.CostEstimate(flops=4 * 10**9, bytes_accessed=12 * MIB, transcendentals=0),
    )(
        here, left_0, left_1, jnp.full((128, 128), 1 / 128, BF16), gain, bias, weight, jnp.asarray(spread, BF16), jnp.asarray(order.reshape(256, 128), BF16),
        w_out, out_gain.reshape(1, 128), out_bias.reshape(1, 128),
    )


def run_gate(first, rows, pair, wide, shift):
    average = jnp.kron(jnp.eye(2, dtype=BF16), jnp.full((128, 128), 1 / 128, BF16))
    return pl.pallas_call(
        functools.partial(gate_kernel, first // 16),
        out_shape=pltpu.HBM((rows, 512, 128), BF16),
        in_specs=[HBM, VMEM, VMEM, VMEM],
        out_specs=HBM,
        compiler_params=pltpu.CompilerParams(vmem_limit_bytes=24 * MIB),
        cost_estimate=pl.CostEstimate(flops=rows * 2 * 10**8, bytes_accessed=MIB, transcendentals=0),
    )(pltpu.with_memory_space_constraint(pair, pltpu.HBM), average, wide, shift)


def place(near, far, x, own, first, other):
    if x == 0:
        if near == 0 or far == 0:
            return own(near, far), 0
        if far != 2:
            return f"{first}{far}", (near - 1) * 16
        return (f"P{first}1", 16 + near * 16) if near < 3 else (f"P{first}3", 32)
    if far == 0:
        if near == 0:
            return "X0", 0
        return (f"{other}3", 64) if near == 3 else ("X2", (near - 1) * 16)
    if far != 2:
        if near == 0:
            return f"{first}{far}", 48
        if near == 2:
            return "X3", 0 if far == 1 else 16
        return f"P{first}{far}", 0 if near == 1 else 16
    if near == 0:
        return f"P{first}3", 48
    return (f"Q{first}1", (near - 1) * 16) if near < 3 else ("X4", 0)


def place_a(z, y, x):
    own = lambda near, far: f"Z{far}" if near == 0 and far else f"Y{near}"
    name, row = place(y, z, x, own, "A", "B")
    return name, row, 0


def place_b(z, y, x):
    own = lambda near, far: f"Y{far}" if near == 0 and far else (f"Z{near}" if near else "Y0")
    name, row = place(z, y, x, own, "B", "A")
    return name, row, 4096 if name[0] in "XYZ" else 0


EARLY = [(z, y, 0) for z in (0, 1, 3) for y in (0, 1, 3)] + [(2, 0, 0), (0, 2, 0)]
EARLY += [(0, 0, 1), (1, 0, 1), (3, 0, 1), (0, 1, 1), (0, 3, 1)]
LATE = [(2, 1, 1), (2, 2, 1), (2, 3, 1), (1, 2, 1), (3, 2, 1)]
OTHERS = [
    (z, y, x)
    for x in range(2)
    for z in range(4)
    for y in range(4)
    if (z, y, x) not in LATE and (z, y, x) not in EARLY
]


def per_device(
    pair_block, left_panel, right_panel, ln_gain, ln_bias, w_left, w_right, w_gate, out_gain, out_bias, w_out
):
    row = lax.axis_index("row")
    z, y, x = row // 8, (row // 2) % 4, row % 2
    c = lax.axis_index("col")

    here = jnp.stack([z, y, x, c]).astype(jnp.int32)

    parts = [lax.dynamic_slice_in_dim(right_panel, ((c + s) % 4) * 16, 16, 0) for s in range(4)]
    parts, weights = lax.optimization_barrier((parts, (ln_gain, ln_bias, w_right, w_gate)))
    gain, bias, weight, wide, shift = run_prepare(*weights)
    pieces = []
    for s in range(4):
        pairs = [(device_id(z_, y_, x_, c_), device_id(c_ + s, y_, x_, z_)) for z_, y_, x_, c_ in DEVICES]
        pieces.append(lax.ppermute(parts[s], AXES, pairs))
    rows = run_right(here, pieces, gain, bias, weight)
    rows, wide, shift = lax.optimization_barrier((rows, wide, shift))
    wide_gate = (wide, shift)

    def cat(*parts):
        return jnp.concatenate(parts, 0)

    got = {}
    def together(*names, more=()):
        held = lax.optimization_barrier([got[n] for n in names] + list(more))
        got.update(zip(names, held))
        return held[len(names) :]

    def call(blocks, before):
        names = sorted({p(*d)[0] for d in blocks for p in (place_a, place_b)})
        found = []
        for d in blocks:
            places = [p(*d) for p in (place_a, place_b)]
            found.append((d, [(names.index(name), row, lane) for name, row, lane in places]))
        sources = [got[n] for n in names]
        return run_update(found, here, sources, gates, lbd, wide_out, shift_out, before)

    def halves(a, b):
        return jnp.concatenate([a, b], 1)

    got["Y0"] = rows
    got["X0"] = move(rows, dx=1)
    for step in (1, 3):
        got[f"Y{step}"], got[f"Z{step}"] = move(rows, dy=-step), move(rows, dz=-step)
    got["Y2"], got["Z2"] = move(got["Y1"], dy=-1), move(got["Z1"], dz=-1)
    got["Y3"], again = lax.optimization_barrier((got["Y3"], left_panel))
    left_2 = move(again, dc=2)
    gate_0 = run_gate(0, GATE_FIRST, pair_block, *wide_gate)
    ones = ("Y1", "Y2", "Y3", "Z1", "Z2", "Z3", "X0")
    (gate_0,) = together(*ones, more=[gate_0])
    half_a = [got[n][:, :4096] for n in ones]
    half_b = [got[n][:, 4096:] for n in ones]
    to_z, to_y = cat(*half_a[:3], half_a[6]), cat(*half_b[3:])
    got["A1"], got["A3"] = move(to_z, dz=-1), move(cat(to_z, half_b[6]), dz=1)
    got["B1"], got["B3"] = move(to_y, dy=-1), move(cat(to_y, half_a[6]), dy=1)
    got["X2"] = move(halves(cat(*half_a[:2]), cat(*half_b[3:5])), dx=1)
    left_0 = jnp.stack([left_panel, left_2])
    left_1 = move(left_0, dc=1)
    gate_1 = run_gate(GATE_FIRST, 64 - GATE_FIRST, pair_block, *wide_gate)
    lbd, wide_out, shift_out = run_left(
        here, left_0, left_1, gain, bias, w_left, w_out, out_gain, out_bias
    )
    gate_1, lbd = together("A1", "A3", "B1", "B3", "X2", more=[gate_1, lbd])
    gates = (gate_0, gate_1)
    a1, a3, b1, b3, x2 = (got[n] for n in ("A1", "A3", "B1", "B3", "X2"))
    xa, xb = cat(x2[:16, :4096], b3[64:]), cat(x2[:16, 4096:], a3[64:])
    got["PA1"], got["PA3"] = move(cat(xa, a1[:32]), dz=-1), move(cat(xa, a3[32:64]), dz=1)
    got["PB1"], got["PB3"] = move(cat(xb, b1[:32]), dy=-1), move(cat(xb, b3[32:64]), dy=1)
    got["X3"] = move(halves(cat(a1[16:32], a3[16:32]), cat(b1[16:32], b3[16:32])), dx=1)
    out = call(EARLY, None)
    (out,) = together("PA1", "PA3", "PB1", "PB3", "X3", more=[out])
    x3 = got["X3"]
    got["QA1"] = move(cat(got["PA1"][:16], x3[:16, :4096]), dz=-1)
    got["QB1"] = move(cat(got["PB1"][:16], x3[:16, 4096:]), dy=-1)
    got["X4"] = move(halves(got["PA3"][32:48], got["PB3"][32:48]), dx=1)
    out = call(OTHERS[:8], out)
    (out,) = together("QA1", "QB1", "X4", more=[out])
    return call(LATE + OTHERS[8:], out)


def solution(mesh):
    part = P("row", "col", None)
    in_specs = (part, part, part) + (P(),) * 8
    return jax.shard_map(per_device, mesh=mesh, in_specs=in_specs, out_specs=part, check_vma=False)
```

```python
import functools

import jax
import jax.numpy as jnp
import numpy as np
from jax import lax
from jax.experimental import pallas as pl
from jax.experimental.pallas import tpu as pltpu
from jax.sharding import PartitionSpec as P

AXES = ("row", "col")
BF16, F32 = jnp.bfloat16, jnp.float32
DEVICES = [(z, y, x, c) for z in range(4) for y in range(4) for x in range(2) for c in range(4)]
MIB = 1 << 20
ENDS = (0, 24, 44, 56, 64)
PARTS = 4
GATE_FIRST = 24


def device_id(z, y, x, c):
    return (((z % 4) * 4 + y % 4) * 2 + x % 2) * 4 + c


def move(value, dz=0, dy=0, dx=0, dc=0):
    pairs = [
        (device_id(z, y, x, c), device_id(z + dz, y + dy, x + dx, c ^ dc)) for z, y, x, c in DEVICES
    ]
    return lax.ppermute(value, AXES, pairs)


def sigmoid(values):
    return 0.5 * jnp.tanh(0.5 * values) + 0.5


def hidden_order():
    order = []
    for group in range(32):
        first = 2 * group
        order += [first, first + 64, first + 1, first + 65]
    return np.array(order)


def standardize(values, average):
    mean = jnp.dot(values, average, preferred_element_type=F32)
    centered = values.astype(F32) - mean
    var = jnp.dot((centered * centered).astype(BF16), average, preferred_element_type=F32)
    return centered * lax.rsqrt(var + 1e-05)


def scale(values, gain, bias):
    return (values * gain.reshape(1, 128) + bias.reshape(1, 128)).astype(BF16)


def project_16(normed, weight, swap, store):
    proj = lax.dot_general(
        weight, normed.reshape(16 * 64, 128), (((0,), (1,)), ((), ())), preferred_element_type=F32
    )
    value = (sigmoid(proj[:128]) * proj[128:]).astype(BF16).astype(F32)
    low, high = value[:64], value[64:]
    lane = lax.broadcasted_iota(jnp.int32, (64, 128), 1)
    for pair in range(8):
        lo = low[:, pair * 128 : (pair + 1) * 128]
        hi = high[:, pair * 128 : (pair + 1) * 128]
        swap[:, 2 * pair, :] = jnp.where(lane < 64, lo, pltpu.roll(hi, 64, 1))
        swap[:, 2 * pair + 1, :] = jnp.where(lane < 64, pltpu.roll(lo, 64, 1), hi)
    for h in range(64):
        store(h, swap[h].astype(BF16))


def prepare_kernel(gain_in, bias_in, right_in, gate_in, gain, bias, right, wide, shift, gain_row, bias_row, gate, sem):
    pairs = ((gain_in, gain_row), (bias_in, bias_row), (right_in, right), (gate_in, gate))
    fetches = [pltpu.make_async_copy(source, target, sem.at[n]) for n, (source, target) in enumerate(pairs)]
    for fetch in fetches:
        fetch.start()
    for fetch in fetches:
        fetch.wait()
    gain[...] = gain_row[...].reshape(1, 128)
    bias[...] = bias_row[...].reshape(1, 128)
    half = 0.5 * gate[...].astype(F32)
    block = (jnp.broadcast_to(gain[...], (128, 128)).T * half).astype(BF16)
    wide[...] = jnp.zeros((256, 256), BF16)
    wide[:128, :128] = block
    wide[128:, 128:] = block
    rows = jnp.broadcast_to(bias[...], (8, 128))
    made = jnp.dot(rows, half, preferred_element_type=F32, precision=lax.Precision.HIGHEST)[:1]
    shift[:, :128] = made
    shift[:, 128:] = made


def right_kernel(here, p0, p1, p2, p3, gain, bias, weight, out, normed, swap):
    average = jnp.full((128, 128), 1 / 128, BF16)
    for s, piece in enumerate((p0, p1, p2, p3)):
        start = pl.multiple_of((here[0] ^ s) * 16, 16)
        made = scale(standardize(piece[...].reshape(256, 128), average), gain[...], bias[...])
        normed[:, pl.ds(start, 16), :] = made.reshape(16, 16, 128)

    def store(h, tile):
        out[:, h * 128 : (h + 1) * 128] = tile

    project_16(normed[...], weight[...], swap, store)


def left_kernel(
    here, left_0, left_1, average, gain, bias, weight, spread, order, w_out, out_gain, out_bias,
    out, wide_out, shift, normed, swap, rows,
):
    for quarter in range(4):
        at = slice(quarter * 16, quarter * 16 + 16)
        mine = normed.at[quarter]
        for flip in range(4):
            piece = (left_0, left_1)[flip % 2][flip // 2, at].reshape(256, 128)
            start = pl.multiple_of((here[3] ^ flip) * 16, 16)
            made = scale(standardize(piece, average[...]), gain[...], bias[...])
            mine[:, pl.ds(start, 16), :] = made.reshape(16, 16, 128)

        def store(h, tile, at=at):
            rows[at, h * 128 : (h + 1) * 128] = tile

        project_16(mine[...], weight[...], swap.at[quarter], store)
    row = lax.broadcasted_iota(jnp.int32, (256, 256), 0)
    lane = lax.broadcasted_iota(jnp.int32, (256, 256), 1)
    keep = lax.rem(row, 4) == lane // 64

    def body(g, carry):
        tile = rows[:, pl.ds(pl.multiple_of(g * 256, 256), 256)]
        wide = jnp.dot(spread[...], tile, preferred_element_type=F32)
        out[g] = jnp.where(keep, wide, 0.0).astype(BF16)
        return carry

    lax.fori_loop(0, 32, body, 0, unroll=32)
    weight_out = w_out[...].astype(F32)
    scaled = jnp.broadcast_to(out_gain[...], (128, 128)).T * weight_out
    made = jnp.dot(order[...], scaled.astype(BF16), preferred_element_type=F32)
    second = lax.rem(lax.broadcasted_iota(jnp.int32, (256, 128), 0), 8) // 4
    wide_out[:, :128] = jnp.where(second == 0, made, 0.0).astype(BF16)
    wide_out[:, 128:] = jnp.where(second == 1, made, 0.0).astype(BF16)
    rows_bias = jnp.broadcast_to(out_bias[...], (8, 128))
    made = jnp.dot(rows_bias, weight_out, preferred_element_type=F32, precision=lax.Precision.HIGHEST)[:1]
    shift[:, :128] = made
    shift[:, 128:] = made


def gate_block(average, weight, bias, pair, out):
    for i in range(0, pair.shape[0], 2):
        both = jnp.concatenate([pair[i], pair[i + 1]], 1)
        mean = jnp.dot(both, average[...], preferred_element_type=F32)
        centered = (both.astype(F32) - mean).astype(BF16)
        var = jnp.dot(centered * centered, average[...], preferred_element_type=F32)
        proj = jnp.dot(centered, weight[...], preferred_element_type=F32)
        proj = proj * lax.rsqrt(var + 1e-05) + bias[...]
        gate = (0.5 * jnp.tanh(proj) + 0.5).astype(BF16)
        out[i], out[i + 1] = gate[:, :128], gate[:, 128:]


def gate_kernel(first, block, pair, average, weight, bias, out):
    rows = out.shape[0]
    spec = pl.BlockSpec((block, 512, 128), lambda n: (n, 0, 0))
    pltpu.emit_pipeline(
        functools.partial(gate_block, average, weight, bias),
        grid=(rows // block,),
        in_specs=[spec],
        out_specs=[spec],
    )(pair.at[pl.ds(first, rows)], out)


def update_kernel(blocks, n_src, has_out, *refs):
    here = refs[0]
    sources = refs[1 : 1 + n_src]
    gate_0, gate_1, lbd, wide_out, shift = refs[1 + n_src : 6 + n_src]
    refs = refs[6 + n_src + has_out :]
    out, product, gates, results, gate_sem, out_sem = refs
    z, y, x = here[0], here[1], here[2]
    columns = 16 * len(blocks)

    def column(b):
        dz, dy, dx = blocks[b][0]
        start = (lax.rem(y + dy, 4) * 2 + lax.rem(x + dx, 2)) * 64 + lax.rem(z + dz, 4) * 16
        return pl.ds(pl.multiple_of(start, 16), 16)

    def gate_copy(b, half):
        return pltpu.make_async_copy(
            (gate_0, gate_1)[half].at[:, column(b), :],
            gates.at[pl.ds(half * GATE_FIRST, (GATE_FIRST, 64 - GATE_FIRST)[half]), pl.ds(b * 16, 16), :],
            gate_sem.at[b, half],
        )

    def out_copy(b, q):
        rows = pl.ds(ENDS[q], ENDS[q + 1] - ENDS[q])
        return pltpu.make_async_copy(
            results.at[rows, pl.ds(b * 16, 16), :], out.at[rows, column(b), :], out_sem.at[b, q]
        )

    for half in range(2):
        for b in range(len(blocks)):
            gate_copy(b, half).start()
    member = lax.broadcasted_iota(jnp.int32, (8, 128), 0)

    def over_four(total):
        swapped = jnp.where(lax.rem(member, 2) == 0, pltpu.roll(total, 7, 0), pltpu.roll(total, 1, 0))
        total = total + swapped
        swapped = jnp.where(lax.rem(member, 4) < 2, pltpu.roll(total, 6, 0), pltpu.roll(total, 2, 0))
        return total + swapped

    for half in range(2):

        def multiply(g, carry, half=half):
            parts = []
            for _, halves in blocks:
                src, row, lane = halves[half]
                at = pl.ds(pl.multiple_of(lane + g * 256, 256), 256)
                parts.append(sources[src][row : row + 16, at])
            made = lax.dot_general(
                lbd[half * 16 + g],
                jnp.concatenate(parts, 0),
                (((1,), (1,)), ((), ())),
                preferred_element_type=F32,
            )
            product[:, half * 16 + g] = made.reshape(32, 8, columns)
            return carry

        lax.fori_loop(0, 16, multiply, 0, unroll=16)
    def finish(ip, carry):
        for part in range(columns // 128):
            lanes = slice(part * 128, part * 128 + 128)
            values = product[ip, :, :, lanes]
            mean = over_four(jnp.sum(values, axis=0)) * (1.0 / 128)
            centered = values - mean[None]
            var = over_four(jnp.sum(centered * centered, axis=0)) * (1.0 / 128)
            normed = centered * lax.rsqrt(var + 1e-05)[None]
            normed = normed.reshape(256, 128).astype(BF16)
            both = lax.dot_general(
                normed, wide_out[...], (((0,), (0,)), ((), ())), preferred_element_type=F32
            )
            both = both + shift[...]
            for i2 in range(2):
                row = 2 * ip + i2
                gate = gates[row, lanes].astype(F32)
                results[row, lanes] = (both[:, i2 * 128 : (i2 + 1) * 128] * gate).astype(BF16)
        return carry

    for q in range(PARTS):
        if q < 2:
            for b in range(len(blocks)):
                gate_copy(b, q).wait()
        lax.fori_loop(ENDS[q] // 2, ENDS[q + 1] // 2, finish, 0, unroll=(ENDS[q + 1] - ENDS[q]) // 2)
        for b in range(len(blocks)):
            out_copy(b, q).start()
    for b in range(len(blocks)):
        for q in range(PARTS):
            out_copy(b, q).wait()


VMEM = pl.BlockSpec(memory_space=pltpu.VMEM)
SMEM = pl.BlockSpec(memory_space=pltpu.SMEM)
HBM = pl.BlockSpec(memory_space=pltpu.HBM)


def run_update(blocks, here, sources, gates, lbd, wide_out, shift, before):
    n = len(blocks)
    has_out = before is not None
    args = [here, *sources, *gates, lbd, wide_out, shift] + ([before] if has_out else [])
    return pl.pallas_call(
        functools.partial(update_kernel, blocks, len(sources), has_out),
        out_shape=pltpu.HBM((64, 512, 128), BF16),
        in_specs=[SMEM] + [VMEM] * len(sources) + [HBM] * 2 + [VMEM] * 3 + [HBM] * has_out,
        out_specs=HBM,
        scratch_shapes=[
            pltpu.VMEM((32, 32, 8, n * 16), F32),
            pltpu.VMEM((64, n * 16, 128), BF16),
            pltpu.VMEM((64, n * 16, 128), BF16),
            pltpu.SemaphoreType.DMA((n, 2)),
            pltpu.SemaphoreType.DMA((n, PARTS)),
        ],
        input_output_aliases={len(args) - 1: 0} if has_out else {},
        compiler_params=pltpu.CompilerParams(vmem_limit_bytes=(8 + 5 * n // 4) * MIB),
        cost_estimate=pl.CostEstimate(flops=n * 4 * 10**8, bytes_accessed=n * MIB, transcendentals=0),
    )(*args)


def run_prepare(*weights):
    weights = [pltpu.with_memory_space_constraint(w, pltpu.HBM) for w in weights]
    return pl.pallas_call(
        prepare_kernel,
        out_shape=[
            jax.ShapeDtypeStruct((1, 128), F32),
            jax.ShapeDtypeStruct((1, 128), F32),
            jax.ShapeDtypeStruct((128, 256), BF16),
            jax.ShapeDtypeStruct((256, 256), BF16),
            jax.ShapeDtypeStruct((1, 256), F32),
        ],
        in_specs=[HBM] * 4,
        out_specs=[VMEM] * 5,
        scratch_shapes=[
            pltpu.VMEM((128,), F32),
            pltpu.VMEM((128,), F32),
            pltpu.VMEM((128, 128), BF16),
            pltpu.SemaphoreType.DMA((4,)),
        ],
        compiler_params=pltpu.CompilerParams(vmem_limit_bytes=4 * MIB),
    )(*weights)


def run_right(here, pieces, gain, bias, weight):
    return pl.pallas_call(
        right_kernel,
        out_shape=jax.ShapeDtypeStruct((16, 8192), BF16),
        in_specs=[SMEM] + [VMEM] * 7,
        out_specs=VMEM,
        scratch_shapes=[pltpu.VMEM((16, 64, 128), BF16), pltpu.VMEM((64, 16, 128), F32)],
        compiler_params=pltpu.CompilerParams(vmem_limit_bytes=8 * MIB),
    )(here, *pieces, gain, bias, weight)


def run_left(here, left_0, left_1, gain, bias, weight, w_out, out_gain, out_bias):
    spread = np.zeros((256, 64), np.float32)
    spread[np.arange(256), np.arange(256) // 4] = 1
    order = np.zeros((32, 2, 4, 128), np.float32)
    for n, h in enumerate(hidden_order()):
        order[n // 4, :, n % 4, h] = 1
    return pl.pallas_call(
        left_kernel,
        out_shape=[
            jax.ShapeDtypeStruct((32, 256, 256), BF16),
            jax.ShapeDtypeStruct((256, 256), BF16),
            jax.ShapeDtypeStruct((1, 256), F32),
        ],
        in_specs=[SMEM] + [VMEM] * 11,
        out_specs=[VMEM] * 3,
        scratch_shapes=[
            pltpu.VMEM((4, 16, 64, 128), BF16),
            pltpu.VMEM((4, 64, 16, 128), F32),
            pltpu.VMEM((64, 8192), BF16),
        ],
        compiler_params=pltpu.CompilerParams(vmem_limit_bytes=20 * MIB),
        cost_estimate=pl.CostEstimate(flops=4 * 10**9, bytes_accessed=12 * MIB, transcendentals=0),
    )(
        here, left_0, left_1, jnp.full((128, 128), 1 / 128, BF16), gain, bias, weight, jnp.asarray(spread, BF16), jnp.asarray(order.reshape(256, 128), BF16),
        w_out, out_gain.reshape(1, 128), out_bias.reshape(1, 128),
    )


def run_gate(first, rows, pair, wide, shift):
    average = jnp.kron(jnp.eye(2, dtype=BF16), jnp.full((128, 128), 1 / 128, BF16))
    return pl.pallas_call(
        functools.partial(gate_kernel, first, rows // 2),
        out_shape=pltpu.HBM((rows, 512, 128), BF16),
        in_specs=[HBM, VMEM, VMEM, VMEM],
        out_specs=HBM,
        compiler_params=pltpu.CompilerParams(vmem_limit_bytes=24 * MIB),
        cost_estimate=pl.CostEstimate(flops=rows * 2 * 10**8, bytes_accessed=MIB, transcendentals=0),
    )(pltpu.with_memory_space_constraint(pair, pltpu.HBM), average, wide, shift)


def place(near, far, x, own, first, other):
    if x == 0:
        if near == 0 or far == 0:
            return own(near, far), 0
        if far != 2:
            return f"{first}{far}", (near - 1) * 16
        return (f"P{first}1", 16 + near * 16) if near < 3 else (f"P{first}3", 32)
    if far == 0:
        if near == 0:
            return "X0", 0
        return (f"{other}3", 64) if near == 3 else ("X2", (near - 1) * 16)
    if far != 2:
        if near == 0:
            return f"{first}{far}", 48
        if near == 2:
            return "X3", 0 if far == 1 else 16
        return f"P{first}{far}", 0 if near == 1 else 16
    if near == 0:
        return f"P{first}3", 48
    return (f"Q{first}1", (near - 1) * 16) if near < 3 else ("X4", 0)


def place_a(z, y, x):
    own = lambda near, far: f"Z{far}" if near == 0 and far else f"Y{near}"
    name, row = place(y, z, x, own, "A", "B")
    return name, row, 0


def place_b(z, y, x):
    own = lambda near, far: f"Y{far}" if near == 0 and far else (f"Z{near}" if near else "Y0")
    name, row = place(z, y, x, own, "B", "A")
    return name, row, 4096 if name[0] in "XYZ" else 0


EARLY = [(z, y, 0) for z in (0, 1, 3) for y in (0, 1, 3)] + [(2, 0, 0), (0, 2, 0)]
EARLY += [(0, 0, 1), (1, 0, 1), (3, 0, 1), (0, 1, 1), (0, 3, 1)]
LATE = [(2, 1, 1), (2, 2, 1), (2, 3, 1), (1, 2, 1), (3, 2, 1)]
OTHERS = [
    (z, y, x)
    for x in range(2)
    for z in range(4)
    for y in range(4)
    if (z, y, x) not in LATE and (z, y, x) not in EARLY
]


def per_device(
    pair_block, left_panel, right_panel, ln_gain, ln_bias, w_left, w_right, w_gate, out_gain, out_bias, w_out
):
    row = lax.axis_index("row")
    z, y, x = row // 8, (row // 2) % 4, row % 2
    c = lax.axis_index("col")

    here = jnp.stack([z, y, x, c]).astype(jnp.int32)

    parts = [lax.dynamic_slice_in_dim(right_panel, (c ^ s) * 16, 16, 0) for s in range(4)]
    parts, weights = lax.optimization_barrier((parts, (ln_gain, ln_bias, w_right, w_gate)))
    gain, bias, weight, wide, shift = run_prepare(*weights)
    pieces = []
    for s in range(4):
        pairs = [(device_id(z_, y_, x_, c_), device_id(c_ ^ s, y_, x_, z_)) for z_, y_, x_, c_ in DEVICES]
        pieces.append(lax.ppermute(parts[s], AXES, pairs))
    rows = run_right(here, pieces, gain, bias, weight)
    rows, wide, shift = lax.optimization_barrier((rows, wide, shift))
    wide_gate = (wide, shift)

    def cat(*parts):
        return jnp.concatenate(parts, 0)

    got = {}
    def together(*names, more=()):
        held = lax.optimization_barrier([got[n] for n in names] + list(more))
        got.update(zip(names, held))
        return held[len(names) :]

    def call(blocks, before):
        names = sorted({p(*d)[0] for d in blocks for p in (place_a, place_b)})
        found = []
        for d in blocks:
            places = [p(*d) for p in (place_a, place_b)]
            found.append((d, [(names.index(name), row, lane) for name, row, lane in places]))
        sources = [got[n] for n in names]
        return run_update(found, here, sources, gates, lbd, wide_out, shift_out, before)

    def halves(a, b):
        return jnp.concatenate([a, b], 1)

    got["Y0"] = rows
    got["X0"] = move(rows, dx=1)
    for step in (1, 3):
        got[f"Y{step}"], got[f"Z{step}"] = move(rows, dy=-step), move(rows, dz=-step)
    got["Y2"], got["Z2"] = move(got["Y1"], dy=-1), move(got["Z1"], dz=-1)
    got["Y3"], again = lax.optimization_barrier((got["Y3"], left_panel))
    left_2 = move(again, dc=2)
    gate_0 = run_gate(0, GATE_FIRST, pair_block, *wide_gate)
    ones = ("Y1", "Y2", "Y3", "Z1", "Z2", "Z3", "X0")
    (gate_0,) = together(*ones, more=[gate_0])
    half_a = [got[n][:, :4096] for n in ones]
    half_b = [got[n][:, 4096:] for n in ones]
    to_z, to_y = cat(*half_a[:3], half_a[6]), cat(*half_b[3:])
    got["A1"], got["A3"] = move(to_z, dz=-1), move(cat(to_z, half_b[6]), dz=1)
    got["B1"], got["B3"] = move(to_y, dy=-1), move(cat(to_y, half_a[6]), dy=1)
    got["X2"] = move(halves(cat(*half_a[:2]), cat(*half_b[3:5])), dx=1)
    left_0 = jnp.stack([left_panel, left_2])
    left_1 = move(left_0, dc=1)
    gate_1 = run_gate(GATE_FIRST, 64 - GATE_FIRST, pair_block, *wide_gate)
    lbd, wide_out, shift_out = run_left(
        here, left_0, left_1, gain, bias, w_left, w_out, out_gain, out_bias
    )
    gate_1, lbd = together("A1", "A3", "B1", "B3", "X2", more=[gate_1, lbd])
    gates = (gate_0, gate_1)
    a1, a3, b1, b3, x2 = (got[n] for n in ("A1", "A3", "B1", "B3", "X2"))
    xa, xb = cat(x2[:16, :4096], b3[64:]), cat(x2[:16, 4096:], a3[64:])
    got["PA1"], got["PA3"] = move(cat(xa, a1[:32]), dz=-1), move(cat(xa, a3[32:64]), dz=1)
    got["PB1"], got["PB3"] = move(cat(xb, b1[:32]), dy=-1), move(cat(xb, b3[32:64]), dy=1)
    got["X3"] = move(halves(cat(a1[16:32], a3[16:32]), cat(b1[16:32], b3[16:32])), dx=1)
    out = call(EARLY, None)
    (out,) = together("PA1", "PA3", "PB1", "PB3", "X3", more=[out])
    x3 = got["X3"]
    got["QA1"] = move(cat(got["PA1"][:16], x3[:16, :4096]), dz=-1)
    got["QB1"] = move(cat(got["PB1"][:16], x3[:16, 4096:]), dy=-1)
    got["X4"] = move(halves(got["PA3"][32:48], got["PB3"][32:48]), dx=1)
    out = call(OTHERS[:8], out)
    (out,) = together("QA1", "QB1", "X4", more=[out])
    return call(LATE + OTHERS[8:], out)


def solution(mesh):
    part = P("row", "col", None)
    in_specs = (part, part, part) + (P(),) * 8
    return jax.shard_map(per_device, mesh=mesh, in_specs=in_specs, out_specs=part, check_vma=False)
```

```python
import functools

import jax
import jax.numpy as jnp
import numpy as np
from jax import lax
from jax.experimental import pallas as pl
from jax.experimental.pallas import tpu as pltpu
from jax.sharding import PartitionSpec as P

AXES = ("row", "col")
BF16, F32 = jnp.bfloat16, jnp.float32
DEVICES = [(z, y, x, c) for z in range(4) for y in range(4) for x in range(2) for c in range(4)]
MIB = 1 << 20
ENDS = (0, 24, 44, 56, 64)
PARTS = 4
GATE_FIRST = 24


def device_id(z, y, x, c):
    return (((z % 4) * 4 + y % 4) * 2 + x % 2) * 4 + c


def move(value, dz=0, dy=0, dx=0, dc=0):
    pairs = [
        (device_id(z, y, x, c), device_id(z + dz, y + dy, x + dx, c ^ dc)) for z, y, x, c in DEVICES
    ]
    return lax.ppermute(value, AXES, pairs)


def sigmoid(values):
    return 0.5 * jnp.tanh(0.5 * values) + 0.5


def hidden_order():
    order = []
    for group in range(32):
        first = 2 * group
        order += [first, first + 64, first + 1, first + 65]
    return np.array(order)


def standardize(values, average):
    mean = jnp.dot(values, average, preferred_element_type=F32)
    centered = values.astype(F32) - mean
    var = jnp.dot((centered * centered).astype(BF16), average, preferred_element_type=F32)
    return centered * lax.rsqrt(var + 1e-05)


def scale(values, gain, bias):
    return (values * gain.reshape(1, 128) + bias.reshape(1, 128)).astype(BF16)


def project_16(normed, weight, swap, store):
    proj = lax.dot_general(
        weight, normed.reshape(16 * 64, 128), (((0,), (1,)), ((), ())), preferred_element_type=F32
    )
    value = (sigmoid(proj[:128]) * proj[128:]).astype(BF16).astype(F32)
    low, high = value[:64], value[64:]
    lane = lax.broadcasted_iota(jnp.int32, (64, 128), 1)
    for pair in range(8):
        lo = low[:, pair * 128 : (pair + 1) * 128]
        hi = high[:, pair * 128 : (pair + 1) * 128]
        swap[:, 2 * pair, :] = jnp.where(lane < 64, lo, pltpu.roll(hi, 64, 1))
        swap[:, 2 * pair + 1, :] = jnp.where(lane < 64, pltpu.roll(lo, 64, 1), hi)
    for h in range(64):
        store(h, swap[h].astype(BF16))


def prepare_kernel(gain_in, bias_in, right_in, gate_in, gain, bias, right, wide, shift, gain_row, bias_row, gate, sem):
    pairs = ((gain_in, gain_row), (bias_in, bias_row), (right_in, right), (gate_in, gate))
    fetches = [pltpu.make_async_copy(source, target, sem.at[n]) for n, (source, target) in enumerate(pairs)]
    for fetch in fetches:
        fetch.start()
    for fetch in fetches:
        fetch.wait()
    gain[...] = gain_row[...].reshape(1, 128)
    bias[...] = bias_row[...].reshape(1, 128)
    half = 0.5 * gate[...].astype(F32)
    block = (jnp.broadcast_to(gain[...], (128, 128)).T * half).astype(BF16)
    wide[...] = jnp.zeros((256, 256), BF16)
    wide[:128, :128] = block
    wide[128:, 128:] = block
    rows = jnp.broadcast_to(bias[...], (8, 128))
    made = jnp.dot(rows, half, preferred_element_type=F32, precision=lax.Precision.HIGHEST)[:1]
    shift[:, :128] = made
    shift[:, 128:] = made


def right_kernel(here, p0, p1, p2, p3, gain, bias, weight, out, normed, swap):
    average = jnp.full((128, 128), 1 / 128, BF16)
    values = jnp.concatenate([piece[...].reshape(256, 128) for piece in (p0, p1, p2, p3)], 0)
    made = scale(standardize(values, average), gain[...], bias[...])
    for s in range(4):
        start = pl.multiple_of((here[0] ^ s) * 16, 16)
        normed[:, pl.ds(start, 16), :] = made[s * 256 : (s + 1) * 256].reshape(16, 16, 128)

    def store(h, tile):
        out[:, h * 128 : (h + 1) * 128] = tile

    project_16(normed[...], weight[...], swap, store)


def left_kernel(
    here, left_0, left_1, average, gain, bias, weight, spread, order, w_out, out_gain, out_bias,
    out, wide_out, shift, normed, swap, rows,
):
    for quarter in range(4):
        at = slice(quarter * 16, quarter * 16 + 16)
        mine = normed.at[quarter]
        for flip in range(4):
            piece = (left_0, left_1)[flip % 2][flip // 2, at].reshape(256, 128)
            start = pl.multiple_of((here[3] ^ flip) * 16, 16)
            made = scale(standardize(piece, average[...]), gain[...], bias[...])
            mine[:, pl.ds(start, 16), :] = made.reshape(16, 16, 128)

        def store(h, tile, at=at):
            rows[at, h * 128 : (h + 1) * 128] = tile

        project_16(mine[...], weight[...], swap.at[quarter], store)
    row = lax.broadcasted_iota(jnp.int32, (256, 256), 0)
    lane = lax.broadcasted_iota(jnp.int32, (256, 256), 1)
    keep = lax.rem(row, 4) == lane // 64

    def body(g, carry):
        tile = rows[:, pl.ds(pl.multiple_of(g * 256, 256), 256)]
        wide = jnp.dot(spread[...], tile, preferred_element_type=F32)
        out[g] = jnp.where(keep, wide, 0.0).astype(BF16)
        return carry

    lax.fori_loop(0, 32, body, 0, unroll=32)
    weight_out = w_out[...].astype(F32)
    scaled = jnp.broadcast_to(out_gain[...], (128, 128)).T * weight_out
    made = jnp.dot(order[...], scaled.astype(BF16), preferred_element_type=F32)
    second = lax.rem(lax.broadcasted_iota(jnp.int32, (256, 128), 0), 8) // 4
    wide_out[:, :128] = jnp.where(second == 0, made, 0.0).astype(BF16)
    wide_out[:, 128:] = jnp.where(second == 1, made, 0.0).astype(BF16)
    rows_bias = jnp.broadcast_to(out_bias[...], (8, 128))
    made = jnp.dot(rows_bias, weight_out, preferred_element_type=F32, precision=lax.Precision.HIGHEST)[:1]
    shift[:, :128] = made
    shift[:, 128:] = made


def gate_block(average, weight, bias, pair, out):
    for i in range(0, pair.shape[0], 2):
        both = jnp.concatenate([pair[i], pair[i + 1]], 1)
        mean = jnp.dot(both, average[...], preferred_element_type=F32)
        centered = (both.astype(F32) - mean).astype(BF16)
        var = jnp.dot(centered * centered, average[...], preferred_element_type=F32)
        proj = jnp.dot(centered, weight[...], preferred_element_type=F32)
        proj = proj * lax.rsqrt(var + 1e-05) + bias[...]
        gate = (0.5 * jnp.tanh(proj) + 0.5).astype(BF16)
        out[i], out[i + 1] = gate[:, :128], gate[:, 128:]


def gate_kernel(first, block, pair, average, weight, bias, out):
    rows = out.shape[0]
    spec = pl.BlockSpec((block, 512, 128), lambda n: (n, 0, 0))
    pltpu.emit_pipeline(
        functools.partial(gate_block, average, weight, bias),
        grid=(rows // block,),
        in_specs=[spec],
        out_specs=[spec],
    )(pair.at[pl.ds(first, rows)], out)


def update_kernel(blocks, n_src, has_out, *refs):
    here = refs[0]
    sources = refs[1 : 1 + n_src]
    gate_0, gate_1, lbd, wide_out, shift = refs[1 + n_src : 6 + n_src]
    refs = refs[6 + n_src + has_out :]
    out, product, gates, results, gate_sem, out_sem = refs
    z, y, x = here[0], here[1], here[2]
    columns = 16 * len(blocks)

    def column(b):
        dz, dy, dx = blocks[b][0]
        start = (lax.rem(y + dy, 4) * 2 + lax.rem(x + dx, 2)) * 64 + lax.rem(z + dz, 4) * 16
        return pl.ds(pl.multiple_of(start, 16), 16)

    def gate_copy(b, half):
        return pltpu.make_async_copy(
            (gate_0, gate_1)[half].at[:, column(b), :],
            gates.at[pl.ds(half * GATE_FIRST, (GATE_FIRST, 64 - GATE_FIRST)[half]), pl.ds(b * 16, 16), :],
            gate_sem.at[b, half],
        )

    def out_copy(b, q):
        rows = pl.ds(ENDS[q], ENDS[q + 1] - ENDS[q])
        return pltpu.make_async_copy(
            results.at[rows, pl.ds(b * 16, 16), :], out.at[rows, column(b), :], out_sem.at[b, q]
        )

    for half in range(2):
        for b in range(len(blocks)):
            gate_copy(b, half).start()
    member = lax.broadcasted_iota(jnp.int32, (8, 128), 0)

    def over_four(total):
        swapped = jnp.where(lax.rem(member, 2) == 0, pltpu.roll(total, 7, 0), pltpu.roll(total, 1, 0))
        total = total + swapped
        swapped = jnp.where(lax.rem(member, 4) < 2, pltpu.roll(total, 6, 0), pltpu.roll(total, 2, 0))
        return total + swapped

    for half in range(2):

        def multiply(g, carry, half=half):
            parts = []
            for _, halves in blocks:
                src, row, lane = halves[half]
                at = pl.ds(pl.multiple_of(lane + g * 256, 256), 256)
                parts.append(sources[src][row : row + 16, at])
            made = lax.dot_general(
                lbd[half * 16 + g],
                jnp.concatenate(parts, 0),
                (((1,), (1,)), ((), ())),
                preferred_element_type=F32,
            )
            product[:, half * 16 + g] = made.reshape(32, 8, columns)
            return carry

        lax.fori_loop(0, 16, multiply, 0, unroll=16)
    def finish(ip, carry):
        for part in range(columns // 128):
            lanes = slice(part * 128, part * 128 + 128)
            values = product[ip, :, :, lanes]
            mean = over_four(jnp.sum(values, axis=0)) * (1.0 / 128)
            centered = values - mean[None]
            var = over_four(jnp.sum(centered * centered, axis=0)) * (1.0 / 128)
            normed = centered * lax.rsqrt(var + 1e-05)[None]
            normed = normed.reshape(256, 128).astype(BF16)
            both = lax.dot_general(
                normed, wide_out[...], (((0,), (0,)), ((), ())), preferred_element_type=F32
            )
            both = both + shift[...]
            for i2 in range(2):
                row = 2 * ip + i2
                gate = gates[row, lanes].astype(F32)
                results[row, lanes] = (both[:, i2 * 128 : (i2 + 1) * 128] * gate).astype(BF16)
        return carry

    for q in range(PARTS):
        if q < 2:
            for b in range(len(blocks)):
                gate_copy(b, q).wait()
        lax.fori_loop(ENDS[q] // 2, ENDS[q + 1] // 2, finish, 0, unroll=(ENDS[q + 1] - ENDS[q]) // 2)
        for b in range(len(blocks)):
            out_copy(b, q).start()
    for b in range(len(blocks)):
        for q in range(PARTS):
            out_copy(b, q).wait()


VMEM = pl.BlockSpec(memory_space=pltpu.VMEM)
SMEM = pl.BlockSpec(memory_space=pltpu.SMEM)
HBM = pl.BlockSpec(memory_space=pltpu.HBM)


def run_update(blocks, here, sources, gates, lbd, wide_out, shift, before):
    n = len(blocks)
    has_out = before is not None
    args = [here, *sources, *gates, lbd, wide_out, shift] + ([before] if has_out else [])
    return pl.pallas_call(
        functools.partial(update_kernel, blocks, len(sources), has_out),
        out_shape=pltpu.HBM((64, 512, 128), BF16),
        in_specs=[SMEM] + [VMEM] * len(sources) + [HBM] * 2 + [VMEM] * 3 + [HBM] * has_out,
        out_specs=HBM,
        scratch_shapes=[
            pltpu.VMEM((32, 32, 8, n * 16), F32),
            pltpu.VMEM((64, n * 16, 128), BF16),
            pltpu.VMEM((64, n * 16, 128), BF16),
            pltpu.SemaphoreType.DMA((n, 2)),
            pltpu.SemaphoreType.DMA((n, PARTS)),
        ],
        input_output_aliases={len(args) - 1: 0} if has_out else {},
        compiler_params=pltpu.CompilerParams(vmem_limit_bytes=(8 + 5 * n // 4) * MIB),
        cost_estimate=pl.CostEstimate(flops=n * 4 * 10**8, bytes_accessed=n * MIB, transcendentals=0),
    )(*args)


def run_prepare(*weights):
    weights = [pltpu.with_memory_space_constraint(w, pltpu.HBM) for w in weights]
    return pl.pallas_call(
        prepare_kernel,
        out_shape=[
            jax.ShapeDtypeStruct((1, 128), F32),
            jax.ShapeDtypeStruct((1, 128), F32),
            jax.ShapeDtypeStruct((128, 256), BF16),
            jax.ShapeDtypeStruct((256, 256), BF16),
            jax.ShapeDtypeStruct((1, 256), F32),
        ],
        in_specs=[HBM] * 4,
        out_specs=[VMEM] * 5,
        scratch_shapes=[
            pltpu.VMEM((128,), F32),
            pltpu.VMEM((128,), F32),
            pltpu.VMEM((128, 128), BF16),
            pltpu.SemaphoreType.DMA((4,)),
        ],
        compiler_params=pltpu.CompilerParams(vmem_limit_bytes=4 * MIB),
    )(*weights)


def run_right(here, pieces, gain, bias, weight):
    return pl.pallas_call(
        right_kernel,
        out_shape=jax.ShapeDtypeStruct((16, 8192), BF16),
        in_specs=[SMEM] + [VMEM] * 7,
        out_specs=VMEM,
        scratch_shapes=[pltpu.VMEM((16, 64, 128), BF16), pltpu.VMEM((64, 16, 128), F32)],
        compiler_params=pltpu.CompilerParams(vmem_limit_bytes=8 * MIB),
    )(here, *pieces, gain, bias, weight)


def run_left(here, left_0, left_1, gain, bias, weight, w_out, out_gain, out_bias):
    spread = np.zeros((256, 64), np.float32)
    spread[np.arange(256), np.arange(256) // 4] = 1
    order = np.zeros((32, 2, 4, 128), np.float32)
    for n, h in enumerate(hidden_order()):
        order[n // 4, :, n % 4, h] = 1
    return pl.pallas_call(
        left_kernel,
        out_shape=[
            jax.ShapeDtypeStruct((32, 256, 256), BF16),
            jax.ShapeDtypeStruct((256, 256), BF16),
            jax.ShapeDtypeStruct((1, 256), F32),
        ],
        in_specs=[SMEM] + [VMEM] * 11,
        out_specs=[VMEM] * 3,
        scratch_shapes=[
            pltpu.VMEM((4, 16, 64, 128), BF16),
            pltpu.VMEM((4, 64, 16, 128), F32),
            pltpu.VMEM((64, 8192), BF16),
        ],
        compiler_params=pltpu.CompilerParams(vmem_limit_bytes=20 * MIB),
        cost_estimate=pl.CostEstimate(flops=4 * 10**9, bytes_accessed=12 * MIB, transcendentals=0),
    )(
        here, left_0, left_1, jnp.full((128, 128), 1 / 128, BF16), gain, bias, weight, jnp.asarray(spread, BF16), jnp.asarray(order.reshape(256, 128), BF16),
        w_out, out_gain.reshape(1, 128), out_bias.reshape(1, 128),
    )


def run_gate(first, rows, pair, wide, shift):
    average = jnp.kron(jnp.eye(2, dtype=BF16), jnp.full((128, 128), 1 / 128, BF16))
    return pl.pallas_call(
        functools.partial(gate_kernel, first, rows // 2),
        out_shape=pltpu.HBM((rows, 512, 128), BF16),
        in_specs=[HBM, VMEM, VMEM, VMEM],
        out_specs=HBM,
        compiler_params=pltpu.CompilerParams(vmem_limit_bytes=24 * MIB),
        cost_estimate=pl.CostEstimate(flops=rows * 2 * 10**8, bytes_accessed=MIB, transcendentals=0),
    )(pltpu.with_memory_space_constraint(pair, pltpu.HBM), average, wide, shift)


def place(near, far, x, own, first, other):
    if x == 0:
        if near == 0 or far == 0:
            return own(near, far), 0
        if far != 2:
            return f"{first}{far}", (near - 1) * 16
        return (f"P{first}1", 16 + near * 16) if near < 3 else (f"P{first}3", 32)
    if far == 0:
        if near == 0:
            return "X0", 0
        return (f"{other}3", 64) if near == 3 else ("X2", (near - 1) * 16)
    if far != 2:
        if near == 0:
            return f"{first}{far}", 48
        if near == 2:
            return "X3", 0 if far == 1 else 16
        return f"P{first}{far}", 0 if near == 1 else 16
    if near == 0:
        return f"P{first}3", 48
    return (f"Q{first}1", (near - 1) * 16) if near < 3 else ("X4", 0)


def place_a(z, y, x):
    own = lambda near, far: f"Z{far}" if near == 0 and far else f"Y{near}"
    name, row = place(y, z, x, own, "A", "B")
    return name, row, 0


def place_b(z, y, x):
    own = lambda near, far: f"Y{far}" if near == 0 and far else (f"Z{near}" if near else "Y0")
    name, row = place(z, y, x, own, "B", "A")
    return name, row, 4096 if name[0] in "XYZ" else 0


EARLY = [(z, y, 0) for z in (0, 1, 3) for y in (0, 1, 3)] + [(2, 0, 0), (0, 2, 0)]
EARLY += [(0, 0, 1), (1, 0, 1), (3, 0, 1), (0, 1, 1), (0, 3, 1)]
LATE = [(2, 1, 1), (2, 2, 1), (2, 3, 1), (1, 2, 1), (3, 2, 1)]
OTHERS = [
    (z, y, x)
    for x in range(2)
    for z in range(4)
    for y in range(4)
    if (z, y, x) not in LATE and (z, y, x) not in EARLY
]


def per_device(
    pair_block, left_panel, right_panel, ln_gain, ln_bias, w_left, w_right, w_gate, out_gain, out_bias, w_out
):
    row = lax.axis_index("row")
    z, y, x = row // 8, (row // 2) % 4, row % 2
    c = lax.axis_index("col")

    here = jnp.stack([z, y, x, c]).astype(jnp.int32)

    parts = [lax.dynamic_slice_in_dim(right_panel, (c ^ s) * 16, 16, 0) for s in range(4)]
    parts, weights = lax.optimization_barrier((parts, (ln_gain, ln_bias, w_right, w_gate)))
    gain, bias, weight, wide, shift = run_prepare(*weights)
    pieces = []
    for s in range(4):
        pairs = [(device_id(z_, y_, x_, c_), device_id(c_ ^ s, y_, x_, z_)) for z_, y_, x_, c_ in DEVICES]
        pieces.append(lax.ppermute(parts[s], AXES, pairs))
    rows = run_right(here, pieces, gain, bias, weight)
    rows, wide, shift = lax.optimization_barrier((rows, wide, shift))
    wide_gate = (wide, shift)

    def cat(*parts):
        return jnp.concatenate(parts, 0)

    got = {}
    def together(*names, more=()):
        held = lax.optimization_barrier([got[n] for n in names] + list(more))
        got.update(zip(names, held))
        return held[len(names) :]

    def call(blocks, before):
        names = sorted({p(*d)[0] for d in blocks for p in (place_a, place_b)})
        found = []
        for d in blocks:
            places = [p(*d) for p in (place_a, place_b)]
            found.append((d, [(names.index(name), row, lane) for name, row, lane in places]))
        sources = [got[n] for n in names]
        return run_update(found, here, sources, gates, lbd, wide_out, shift_out, before)

    def halves(a, b):
        return jnp.concatenate([a, b], 1)

    got["Y0"] = rows
    got["X0"] = move(rows, dx=1)
    for step in (1, 3):
        got[f"Y{step}"], got[f"Z{step}"] = move(rows, dy=-step), move(rows, dz=-step)
    got["Y2"], got["Z2"] = move(got["Y1"], dy=-1), move(got["Z1"], dz=-1)
    got["Y3"], again = lax.optimization_barrier((got["Y3"], left_panel))
    left_2 = move(again, dc=2)
    gate_0 = run_gate(0, GATE_FIRST, pair_block, *wide_gate)
    ones = ("Y1", "Y2", "Y3", "Z1", "Z2", "Z3", "X0")
    (gate_0,) = together(*ones, more=[gate_0])
    half_a = [got[n][:, :4096] for n in ones]
    half_b = [got[n][:, 4096:] for n in ones]
    to_z, to_y = cat(*half_a[:3], half_a[6]), cat(*half_b[3:])
    got["A1"], got["A3"] = move(to_z, dz=-1), move(cat(to_z, half_b[6]), dz=1)
    got["B1"], got["B3"] = move(to_y, dy=-1), move(cat(to_y, half_a[6]), dy=1)
    got["X2"] = move(halves(cat(*half_a[:2]), cat(*half_b[3:5])), dx=1)
    left_0 = jnp.stack([left_panel, left_2])
    left_1 = move(left_0, dc=1)
    gate_1 = run_gate(GATE_FIRST, 64 - GATE_FIRST, pair_block, *wide_gate)
    lbd, wide_out, shift_out = run_left(
        here, left_0, left_1, gain, bias, w_left, w_out, out_gain, out_bias
    )
    gate_1, lbd = together("A1", "A3", "B1", "B3", "X2", more=[gate_1, lbd])
    gates = (gate_0, gate_1)
    a1, a3, b1, b3, x2 = (got[n] for n in ("A1", "A3", "B1", "B3", "X2"))
    xa, xb = cat(x2[:16, :4096], b3[64:]), cat(x2[:16, 4096:], a3[64:])
    got["PA1"], got["PA3"] = move(cat(xa, a1[:32]), dz=-1), move(cat(xa, a3[32:64]), dz=1)
    got["PB1"], got["PB3"] = move(cat(xb, b1[:32]), dy=-1), move(cat(xb, b3[32:64]), dy=1)
    got["X3"] = move(halves(cat(a1[16:32], a3[16:32]), cat(b1[16:32], b3[16:32])), dx=1)
    out = call(EARLY, None)
    (out,) = together("PA1", "PA3", "PB1", "PB3", "X3", more=[out])
    x3 = got["X3"]
    got["QA1"] = move(cat(got["PA1"][:16], x3[:16, :4096]), dz=-1)
    got["QB1"] = move(cat(got["PB1"][:16], x3[:16, 4096:]), dy=-1)
    got["X4"] = move(halves(got["PA3"][32:48], got["PB3"][32:48]), dx=1)
    out = call(OTHERS[:8], out)
    (out,) = together("QA1", "QB1", "X4", more=[out])
    return call(LATE + OTHERS[8:], out)


def solution(mesh):
    part = P("row", "col", None)
    in_specs = (part, part, part) + (P(),) * 8
    return jax.shard_map(per_device, mesh=mesh, in_specs=in_specs, out_specs=part, check_vma=False)
```
